128 devices in a mesh: lat: 16 (over z, y), chan: 8 (over x, core).
Axes of the slice: x: 4, y: 4, z: 4, core: 2. Of those that a mesh axis runs over, the one named last changes fastest.
Arguments:
- grid_in: bfloat16 [1, 720, 256, 1440], P(None, 'lat', 'chan'), may hold values from -6 to 6
- lat_weights: float32 [720], P('lat'), may hold values from 0.25 to 4
- legendre_basis: bfloat16 [192, 385, 720], P('lat'), may hold values from -0.21875 to 0.21875
- pair_list: int32 [192], replicated, may hold values from 0 to 191, each once
- filter_weights: bfloat16 [384, 256, 256], P(None, 'chan'), may hold values from -0.375 to 0.375
- cotangent: bfloat16 [1, 720, 256, 1440], P(None, 'lat', 'chan'), may hold values from -6 to 6
Outputs:
- block_out: bfloat16 [1, 720, 256, 1440], P(None, 'lat', 'chan')
- weight_grad: float32 [384, 256, 256], P('lat', 'chan')
The draws below stay inside these ranges and needn't reach their ends.
Inputs may be any that keep to these rules, and one draw needn't show every extreme that they name: pair_list holds each of the 192 pairs of orders once; slot k pairs order pair_list[k] with order 384 - 1 - pair_list[k].
All inputs are finite; a program needn't handle non-finite values.
Results may differ from the reference program's by a relative error of at most 0.033.
Values may be sent and summed in bfloat16 or wider, within the bound.
No kernel may reach another device: no remote copies, remote signals or barrier semaphores. Data moves between devices by JAX's collectives and lax.ppermute only.
A program may use at most 192 MiB of HBM per device.

```python
import math
import jax
import jax.numpy as jnp
from jax import lax

B = 1
NLAT = 720
NLON = 1440
C = 256
L = 384
PAIRS = 192


def block_scale(key, shape, pieces, low, high):
    def one(dim, shards_of):
        heights = jax.random.uniform(jax.random.fold_in(jax.random.fold_in(key, 6), dim), (shards_of,), jnp.float32, low / len(pieces), high / len(pieces))
        return jnp.repeat(jnp.exp(heights), shape[dim] // shards_of).reshape((-1,) + (1,) * (len(shape) - dim - 1))

    loudness = one(*pieces[0])
    for cut in pieces[1:]:
        loudness = loudness * one(*cut)
    return loudness


def normal_values(rng, dims, scale, bound, pieces=(), kind=jnp.bfloat16):
    drawn = scale * jax.random.normal(rng, dims, jnp.float32)
    if pieces:
        drawn = drawn * block_scale(rng, dims, pieces, -0.22, 0.18)
    return jnp.clip(drawn, -bound, bound).astype(kind)


def setup_inputs(seed: int = 0) -> dict:
    splits = jax.random.split(jax.random.key(seed), 7)
    return {
        "grid_in": normal_values(splits[0], (B, NLAT, C, NLON), 1.0, 6.0, ((1, 16), (2, 8))),
        "lat_weights": jnp.clip(jnp.exp(math.log(4.0) - 2.7725887 * jax.random.uniform(splits[1], (NLAT,), jnp.float32) ** block_scale(splits[1], (NLAT,), ((0, 16),), -0.2, 0.2)), 0.25, 4.0),
        "legendre_basis": normal_values(splits[2], (PAIRS, L + 1, NLAT), NLAT ** -0.5, 0.21875, ((0, 16),)),
        "pair_list": jax.random.permutation(splits[3], PAIRS).astype(jnp.int32),
        "filter_weights": normal_values(splits[4], (L, C, C), C ** -0.5, 0.375, ((1, 8),)),
        "cotangent": normal_values(splits[5], (B, NLAT, C, NLON), 1.0, 6.0, ((1, 16), (2, 8))),
    }


def analysis(legendre_basis, spectra, first_orders):
    products = jnp.einsum('krt,btckwi->krwibc', legendre_basis.astype(jnp.float32), spectra.astype(jnp.float32), precision=lax.Precision.HIGHEST)
    row_index = jnp.arange(L + 1, dtype=jnp.int32)
    upper_rows = row_index[None, :] < (L - first_orders)[:, None]
    return jnp.where(upper_rows[:, :, None, None, None], products[:, :, 0], products[:, :, 1])

def degree_table(packed, first_orders):

    def lower_part(block_rows, offset):
        padded = jnp.concatenate([jnp.zeros((L,) + block_rows.shape[1:], block_rows.dtype), block_rows], axis=0)
        return lax.dynamic_slice_in_dim(padded, (L - offset).astype(jnp.int32), L, 0)
    leading = jax.vmap(lower_part)(packed, first_orders)
    degree_index = jnp.arange(L, dtype=jnp.int32)
    keep_rows = degree_index[None, :] >= (L - 1 - first_orders)[:, None]
    trailing = jnp.where(keep_rows[:, :, None, None, None], packed[:, 1:], jnp.zeros((), packed.dtype))
    return jnp.stack([leading, trailing], axis=1)

def packed_table(by_degree, first_orders):

    def upper_part(block_rows, offset):
        padded = jnp.concatenate([block_rows, jnp.zeros((L + 1,) + block_rows.shape[1:], block_rows.dtype)], axis=0)
        return lax.dynamic_slice_in_dim(padded, offset.astype(jnp.int32), L + 1, 0)
    leading = jax.vmap(upper_part)(by_degree[:, 0], first_orders)
    trailing = by_degree[:, 1]
    trailing = jnp.concatenate([jnp.zeros_like(trailing[:, :1]), trailing], axis=1)
    return jnp.stack([leading, trailing], axis=1)

def reference(grid_in, lat_weights, legendre_basis, pair_list, filter_weights, cotangent):
    first_orders = pair_list.astype(jnp.int32)
    orders = jnp.stack([first_orders, L - 1 - first_orders], axis=1).reshape(-1)
    lon_scale = 1.0 / math.sqrt(NLON)
    signal = grid_in.astype(jnp.float32)
    transform = jnp.fft.rfft(signal, axis=-1)[..., :L] * lon_scale
    weights = lat_weights.astype(jnp.float32)[None, :, None, None]
    spectrum = jnp.stack([jnp.real(transform) * weights, jnp.imag(transform) * weights], axis=-1).astype(jnp.bfloat16)
    spectra = spectrum[:, :, :, orders, :].reshape(B, NLAT, C, PAIRS, 2, 2)
    coefficients = analysis(legendre_basis, spectra, first_orders).astype(jnp.bfloat16)
    by_degree = degree_table(coefficients, first_orders)
    filtered = jnp.einsum('loc,kwlibc->kwlibo', filter_weights.astype(jnp.float32), by_degree.astype(jnp.float32), precision=lax.Precision.HIGHEST).astype(jnp.bfloat16)
    rows_packed = packed_table(filtered, first_orders)
    synthesis = jnp.einsum('krt,kwribo->btokwi', legendre_basis.astype(jnp.float32), rows_packed.astype(jnp.float32), precision=lax.Precision.HIGHEST).astype(jnp.bfloat16)
    columns = synthesis.reshape(B, NLAT, C, L, 2)
    inverse_index = jnp.zeros((L,), jnp.int32).at[orders].set(jnp.arange(L, dtype=jnp.int32))
    by_order = columns[:, :, :, inverse_index, :].astype(jnp.float32)
    full_spectrum = lax.complex(by_order[..., 0], by_order[..., 1])
    full_spectrum = jnp.pad(full_spectrum, ((0, 0), (0, 0), (0, 0), (0, NLON // 2 + 1 - L)))
    grid_field = jnp.fft.irfft(full_spectrum, n=NLON, axis=-1) * math.sqrt(NLON)
    block_out = (signal + jax.nn.gelu(grid_field)).astype(jnp.bfloat16)
    pullback = jax.vjp(jax.nn.gelu, grid_field)[1]
    field_grad = pullback(cotangent.astype(jnp.float32))[0].astype(jnp.bfloat16)
    factor = jnp.where(jnp.arange(L) == 0, 1.0, 2.0).astype(jnp.float32) * lon_scale
    grad_transform = jnp.fft.rfft(field_grad.astype(jnp.float32), axis=-1)[..., :L]
    grad_spectrum = jnp.stack([jnp.real(grad_transform) * factor, jnp.imag(grad_transform) * factor], axis=-1).astype(jnp.bfloat16)
    grad_spectra = grad_spectrum[:, :, :, orders, :].reshape(B, NLAT, C, PAIRS, 2, 2)
    coefficient_grad = analysis(legendre_basis, grad_spectra, first_orders).astype(jnp.bfloat16)
    degree_grad = degree_table(coefficient_grad, first_orders)
    weight_grad = jnp.einsum('kwlibo,kwlibc->loc', degree_grad.astype(jnp.float32), by_degree.astype(jnp.float32), precision=lax.Precision.HIGHEST)
    return (block_out, weight_grad)
```

```python
import functools
import math

import jax
import jax.numpy as jnp
import numpy as np
from jax import lax
from jax.experimental import pallas as pl
from jax.experimental.pallas import tpu as pltpu
from jax.sharding import PartitionSpec as P

F32 = jnp.float32
BF16 = jnp.bfloat16
GROUP = 32
T_STEP = 16
CHUNKS = ((0, 12),)


def params(mib=56):
    return pltpu.CompilerParams(vmem_limit_bytes=mib << 20)


def round_up(value, unit):
    return -(-value // unit) * unit


def longitude_table(degrees, lon_count, doubled):
    first = np.arange(degrees // 2)
    orders = np.stack([first, degrees - 1 - first])
    phases = orders[:, :, None] * np.arange(lon_count) % lon_count
    angles = phases * (2.0 * math.pi / lon_count)
    table = np.stack([np.cos(angles), -np.sin(angles)], axis=1) / math.sqrt(lon_count)
    if doubled:
        table = table * np.where(orders == 0, 1.0, 2.0)[:, None, :, None]
    return jnp.asarray(table.reshape(2 * degrees, lon_count).astype(np.float32)).astype(BF16)


def swap_groups(tiles):
    lane_group = lax.broadcasted_iota(jnp.int32, tiles[0].shape, 1) // GROUP
    swapped = []
    for s in range(4):
        total = None
        for a in range(4):
            shift = (a - s) % 4 * GROUP
            moved = pltpu.roll(tiles[a], shift, 1) if shift else tiles[a]
            total = moved if total is None else jnp.where(lane_group == a, moved, total)
        swapped.append(total)
    return swapped


P_BLOCK = 32


def by_latitude(rows_ref, stacked_ref, pairs, scale_ref):
    def step(block, _):
        start = pl.multiple_of(block * P_BLOCK, P_BLOCK)
        for q in range(T_STEP // 4):
            lanes = slice(128 * q, 128 * q + 128)
            tiles = [rows_ref[pl.ds(wi * pairs + start, P_BLOCK), lanes] for wi in range(4)]
            if scale_ref is not None:
                tiles = [tile * scale_ref[:, lanes] for tile in tiles]
            for s, tile in enumerate(swap_groups(tiles)):
                stacked_ref[pl.ds((4 * q + s) * pairs + start, P_BLOCK), :] = tile
        return 0

    lax.fori_loop(0, pairs // P_BLOCK, step, 0)


def by_order(stacked_ref, rows_ref, pairs):
    def step(block, _):
        start = pl.multiple_of(block * P_BLOCK, P_BLOCK)
        for q in range(T_STEP // 4):
            tiles = [
                stacked_ref[pl.ds((4 * q + s) * pairs + start, P_BLOCK), :] for s in range(4)
            ]
            for wi, tile in enumerate(swap_groups(tiles)):
                rows_ref[pl.ds(wi * pairs + start, P_BLOCK), 128 * q : 128 * q + 128] = tile.astype(
                    rows_ref.dtype
                )
        return 0

    lax.fori_loop(0, pairs // P_BLOCK, step, 0)


def send_slots(pair_ref, stacked_ref, out_refs, pairs, slots):
    for (low, high), out_ref in zip(CHUNKS, out_refs):

        def step(owner, _):
            for k in range(low, high):
                order = pair_ref[owner * slots + k]
                tile = stacked_ref[pl.ds(order, T_STEP, stride=pairs), :]
                out_ref[owner, k - low] = tile.astype(BF16)
            return 0

        lax.fori_loop(0, pairs // slots, step, 0)


def nt_dot(a, b):
    return lax.dot_general(a, b, (((1,), (1,)), ((), ())), preferred_element_type=F32)


def tn_dot(a, b):
    return lax.dot_general(a, b, (((0,), (0,)), ((), ())), preferred_element_type=F32)


def forward_body(pairs, slots, pair_ref, grid_ref, scale_ref, table_ref, *refs):
    out_refs = refs[: len(CHUNKS)]
    rows_ref, stacked_ref = refs[len(CHUNKS) :]
    fields = grid_ref[...].reshape(T_STEP * GROUP, -1)
    rows_ref[...] = nt_dot(table_ref[...], fields)
    by_latitude(rows_ref, stacked_ref, pairs, scale_ref)
    send_slots(pair_ref, stacked_ref, out_refs, pairs, slots)


def slot_specs(owners):
    return [
        pl.BlockSpec((owners, high - low, T_STEP, 128), lambda t: (0, 0, t, 0))
        for low, high in CHUNKS
    ]


def slot_shapes(owners, lat_rows):
    return [jax.ShapeDtypeStruct((owners, high - low, lat_rows, 128), BF16) for low, high in CHUNKS]


def forward_transform(grid, scale, pair_list, table, owners, slots):
    lat_rows, _, lon_count = grid.shape
    pairs = owners * slots
    return pl.pallas_call(
        functools.partial(forward_body, pairs, slots),
        grid=(pl.cdiv(lat_rows, T_STEP),),
        in_specs=[
            pl.BlockSpec(memory_space=pltpu.SMEM),
            pl.BlockSpec((T_STEP, GROUP, lon_count), lambda t: (t, 0, 0)),
            pl.BlockSpec((1, T_STEP * GROUP), lambda t: (0, t)),
            pl.BlockSpec((4 * pairs, lon_count), lambda t: (0, 0)),
        ],
        out_specs=slot_specs(owners),
        out_shape=slot_shapes(owners, lat_rows),
        scratch_shapes=[
            pltpu.VMEM((4 * pairs, T_STEP * GROUP), F32),
            pltpu.VMEM((T_STEP * pairs, 128), F32),
        ],
        compiler_params=params(),
        name="forward_transform",
    )(pair_list, grid, scale, table)


def middle_body(pairs, slots, pair_ref, *refs):
    count = len(CHUNKS)
    in_refs, refs = refs[:count], refs[count:]
    grid_ref, cot_ref, table_ref, out_ref = refs[:4]
    out_refs = refs[4 : 4 + count]
    rows_ref, stacked_ref, lines_ref, grad_ref = refs[4 + count :]
    for (low, high), in_ref in zip(CHUNKS, in_refs):

        def step(owner, _):
            for k in range(low, high):
                order = pair_ref[owner * slots + k]
                tile = in_ref[owner, k - low].astype(F32)
                stacked_ref[pl.ds(order, T_STEP, stride=pairs), :] = tile
            return 0

        lax.fori_loop(0, pairs // slots, step, 0)
    by_order(stacked_ref, lines_ref, pairs)
    root = math.sqrt(2.0 / math.pi)
    t_part = 4
    for q in range(T_STEP // t_part):
        rows = slice(128 * q, 128 * q + 128)
        lats = slice(t_part * q, t_part * q + t_part)
        x = tn_dot(lines_ref[:, rows], table_ref[...])
        square = x * x
        th = jnp.tanh(x * (root + (root * 0.044715) * square))
        half = 0.5 + 0.5 * th
        gate = x * half
        slope = half + gate * (1.0 - th) * (root + (3.0 * root * 0.044715) * square)
        grid = grid_ref[lats].reshape(128, -1).astype(F32)
        out_ref[lats] = (grid + gate).astype(BF16).reshape(t_part, GROUP, -1)
        cot = cot_ref[lats].reshape(128, -1).astype(F32)
        grad_ref[rows, :] = (cot * slope).astype(BF16)
    rows_ref[...] = nt_dot(table_ref[...], grad_ref[...])
    by_latitude(rows_ref, stacked_ref, pairs, None)
    send_slots(pair_ref, stacked_ref, out_refs, pairs, slots)


def middle_transform(returned, grid, cotangent, pair_list, table, owners, slots):
    lat_rows, _, lon_count = grid.shape
    pairs = owners * slots
    field_spec = pl.BlockSpec((T_STEP, GROUP, lon_count), lambda t: (t, 0, 0))
    return pl.pallas_call(
        functools.partial(middle_body, pairs, slots),
        grid=(pl.cdiv(lat_rows, T_STEP),),
        in_specs=[pl.BlockSpec(memory_space=pltpu.SMEM)]
        + slot_specs(owners)
        + [
            field_spec,
            field_spec,
            pl.BlockSpec((4 * pairs, lon_count), lambda t: (0, 0)),
        ],
        out_specs=[field_spec] + slot_specs(owners),
        out_shape=[jax.ShapeDtypeStruct(grid.shape, BF16)] + slot_shapes(owners, lat_rows),
        scratch_shapes=[
            pltpu.VMEM((4 * pairs, T_STEP * GROUP), F32),
            pltpu.VMEM((T_STEP * pairs, 128), F32),
            pltpu.VMEM((4 * pairs, T_STEP * GROUP), BF16),
            pltpu.VMEM((T_STEP * GROUP, lon_count), BF16),
        ],
        compiler_params=params(),
        name="middle_transform",
    )(pair_list, *returned, grid, cotangent, table)


def degree_starts(degrees, chans, block_rows, count):
    starts = []
    for tile in range(degrees // 8):
        owner, s = divmod(tile, degrees // 8 // 16)
        starts.append(owner * chans * block_rows + s * count)
    return starts


def analysis_body(degrees, low, count, block_rows, first_ref, in_ref, basis_ref, out_ref, *refs):
    lats_ref, rows_ref, sent_ref = refs
    k = pl.program_id(0)
    first = first_ref[low + k]
    owners, lat_rows = in_ref.shape[0], in_ref.shape[2]

    @pl.when(k == 0)
    def _():
        sent_ref[...] = jnp.zeros_like(sent_ref)

    for owner in range(owners):
        lats_ref[owner * lat_rows : (owner + 1) * lat_rows, :] = in_ref[owner, 0].astype(F32)
    spectrum = lats_ref[...].astype(BF16)
    rows_ref[: degrees + 1, :] = jnp.dot(basis_ref[0], spectrum, preferred_element_type=F32)
    rows_ref[degrees + 1 :, :] = jnp.zeros((7, 128), F32)
    leading = pltpu.roll(rows_ref[...], first, 0)[:degrees]
    trailing = rows_ref[1 : degrees + 1, :]
    degree = lax.broadcasted_iota(jnp.int32, (degrees, 128), 0)
    lane = lax.broadcasted_iota(jnp.int32, (degrees, 128), 1)
    is_first = lane < 64
    smallest = jnp.where(is_first, first, degrees - 1 - first)
    table = jnp.where(degree >= smallest, jnp.where(is_first, leading, trailing), 0.0)
    for tile, start in enumerate(degree_starts(degrees, 8, block_rows, count)):
        sent_ref[pl.ds(start + k, 8, stride=block_rows), :] = table[8 * tile : 8 * tile + 8]

    @pl.when(k == pl.num_programs(0) - 1)
    def _():
        out_ref[...] = sent_ref[...].astype(BF16).reshape(out_ref.shape)


def analysis(arrived, basis, firsts, chunk):
    low, high = chunk
    count = high - low
    owners, _, lat_rows, _ = arrived.shape
    slots, rows, lat_total = basis.shape
    degrees = rows - 1
    block_rows = round_up(3 * count, 8)
    return pl.pallas_call(
        functools.partial(analysis_body, degrees, low, count, block_rows),
        grid=(count,),
        in_specs=[
            pl.BlockSpec(memory_space=pltpu.SMEM),
            pl.BlockSpec((owners, 1, lat_rows, 128), lambda k: (0, k, 0, 0)),
            pl.BlockSpec((1, rows, lat_total), lambda k: (low + k, 0, 0)),
        ],
        out_specs=pl.BlockSpec((128, block_rows, 128), lambda k: (0, 0, 0)),
        out_shape=jax.ShapeDtypeStruct((128, block_rows, 128), BF16),
        scratch_shapes=[
            pltpu.VMEM((lat_total, 128), F32),
            pltpu.VMEM((degrees + 8, 128), F32),
            pltpu.VMEM((128 * block_rows, 128), F32),
        ],
        compiler_params=params(),
        name="analysis",
    )(firsts, arrived, basis)


def synthesis_body(degrees, low, count, block_rows, first_ref, in_ref, basis_ref, out_ref, *refs):
    held_ref, rows_ref, lats_ref = refs
    k = pl.program_id(0)
    first = first_ref[low + k]
    owners, lat_rows = out_ref.shape[0], out_ref.shape[2]

    @pl.when(k == 0)
    def _():
        held_ref[...] = in_ref[...].astype(F32).reshape(held_ref.shape)
        rows_ref[...] = jnp.zeros_like(rows_ref)

    for tile, start in enumerate(degree_starts(degrees, 8, block_rows, count)):
        rows_ref[8 * tile : 8 * tile + 8, :] = held_ref[pl.ds(start + k, 8, stride=block_rows), :]
    table = rows_ref[...]
    size = degrees + 8
    leading = pltpu.roll(table, lax.rem(size - first, size), 0)
    trailing = pltpu.roll(table, 1, 0)
    row = lax.broadcasted_iota(jnp.int32, (size, 128), 0)
    is_first = lax.broadcasted_iota(jnp.int32, (size, 128), 1) < 64
    lines = jnp.where(
        row < degrees - first,
        jnp.where(is_first, leading, 0.0),
        jnp.where(is_first, 0.0, trailing),
    )
    lats_ref[...] = tn_dot(basis_ref[0], lines[: degrees + 1].astype(BF16))
    for owner in range(owners):
        out_ref[owner, 0] = lats_ref[owner * lat_rows : (owner + 1) * lat_rows, :].astype(BF16)


def synthesize(filtered, basis, firsts, chunk, owners, lat_rows):
    low, high = chunk
    count = high - low
    slots, rows, lat_total = basis.shape
    degrees = rows - 1
    block_rows = filtered.shape[1]
    return pl.pallas_call(
        functools.partial(synthesis_body, degrees, low, count, block_rows),
        grid=(count,),
        in_specs=[
            pl.BlockSpec(memory_space=pltpu.SMEM),
            pl.BlockSpec((128, block_rows, 128), lambda k: (0, 0, 0)),
            pl.BlockSpec((1, rows, lat_total), lambda k: (low + k, 0, 0)),
        ],
        out_specs=pl.BlockSpec((owners, 1, lat_rows, 128), lambda k: (0, k, 0, 0)),
        out_shape=jax.ShapeDtypeStruct((owners, count, lat_rows, 128), BF16),
        scratch_shapes=[
            pltpu.VMEM((128 * block_rows, 128), F32),
            pltpu.VMEM((degrees + 8, 128), F32),
            pltpu.VMEM((lat_total, 128), F32),
        ],
        compiler_params=params(),
        name="synthesis",
    )(firsts, filtered, basis)


def gather_channels(in_ref, rows_ref, block_rows):
    def step(owner, _):
        start = pl.multiple_of(owner * block_rows, 8)
        for half in range(2):
            tiles = [in_ref[owner * 8 + 4 * half + a].astype(F32) for a in range(4)]
            for hj, tile in enumerate(swap_groups(tiles)):
                rows_ref[hj, pl.ds(start, block_rows), 128 * half : 128 * half + 128] = tile
        return 0

    lax.fori_loop(0, in_ref.shape[0] // 8, step, 0)


def row_degrees(block_rows, count, total):
    row = lax.broadcasted_iota(jnp.int32, (total // block_rows, block_rows, 256), 1)
    row = row.reshape(total, 256)
    return (row >= count).astype(jnp.int32) + (row >= 2 * count).astype(jnp.int32)


def filter_body(count, block_rows, in_ref, weight_ref, out_ref, degree_ref, rows_ref):
    gather_channels(in_ref, rows_ref, block_rows)
    total = rows_ref.shape[1]
    which = row_degrees(block_rows, count, total)
    weights = [weight_ref[:, s].reshape(256, 256) for s in range(3)]
    for hj in range(4):
        table = rows_ref[hj].astype(BF16)
        degree_ref[hj] = table
        kept = nt_dot(table, weights[0])
        kept = jnp.where(which == 1, nt_dot(table, weights[1]), kept)
        rows_ref[hj] = jnp.where(which == 2, nt_dot(table, weights[2]), kept)

    def step(owner, _):
        start = pl.multiple_of(owner * block_rows, 8)
        for half in range(2):
            tiles = [
                rows_ref[hj, pl.ds(start, block_rows), 128 * half : 128 * half + 128]
                for hj in range(4)
            ]
            for a, tile in enumerate(swap_groups(tiles)):
                out_ref[owner * 8 + 4 * half + a] = tile.astype(BF16)
        return 0

    lax.fori_loop(0, out_ref.shape[0] // 8, step, 0)


def spectral_filter(received, weights, count):
    devices, block_rows, _ = received.shape
    total = devices // 8 * block_rows
    return pl.pallas_call(
        functools.partial(filter_body, count, block_rows),
        out_shape=[
            jax.ShapeDtypeStruct(received.shape, BF16),
            jax.ShapeDtypeStruct((4, total, 256), BF16),
        ],
        scratch_shapes=[pltpu.VMEM((4, total, 256), F32)],
        compiler_params=params(),
        name="spectral_filter",
    )(received, weights)


def grad_body(counts, *refs):
    parts = len(counts)
    in_refs, degree_refs = refs[:parts], refs[parts : 2 * parts]
    out_ref = refs[2 * parts]
    scratch = refs[2 * parts + 1 :]
    sums = [None] * 3
    for count, in_ref, degree_ref, rows_ref in zip(counts, in_refs, degree_refs, scratch):
        block_rows = in_ref.shape[1]
        gather_channels(in_ref, rows_ref, block_rows)
        total = rows_ref.shape[1]
        which = row_degrees(block_rows, count, total)
        for hj in range(4):
            grad = rows_ref[hj]
            for s in range(3):
                term = tn_dot(jnp.where(which == s, grad, 0.0).astype(BF16), degree_ref[hj])
                sums[s] = term if sums[s] is None else sums[s] + term
    for s in range(3):
        out_ref[:, s] = sums[s].astype(BF16).reshape(8, GROUP, 256)


def filter_grad(received, by_degree, counts):
    return pl.pallas_call(
        functools.partial(grad_body, counts),
        out_shape=jax.ShapeDtypeStruct((8, 3, GROUP, 256), BF16),
        scratch_shapes=[pltpu.VMEM(table.shape, F32) for table in by_degree],
        compiler_params=params(),
        name="filter_grad",
    )(*received, *by_degree)


def exchange(array, axis):
    return lax.all_to_all(array, axis, split_axis=0, concat_axis=0, tiled=True)


def on_device(grid_in, lat_weights, legendre_basis, pair_list, filter_weights, cotangent):
    owners = lax.axis_size("lat")
    chans = lax.axis_size("chan")
    owner_index = lax.axis_index("lat")
    slots, rows, _ = legendre_basis.shape
    degrees = rows - 1
    _, lat_rows, chan_rows, lon_count = grid_in.shape
    grid, cotangent = grid_in[0], cotangent[0]
    firsts = lax.dynamic_slice_in_dim(pair_list, owner_index * slots, slots)
    scale = jnp.repeat(lat_weights, GROUP).reshape(1, -1)
    degrees_here = degrees // owners
    weights = lax.dynamic_slice_in_dim(filter_weights, owner_index * degrees_here, degrees_here, 0)
    weights = weights.reshape(degrees_here // chans, chans, chan_rows, -1).swapaxes(0, 1)
    weights = exchange(weights, "chan")
    table = longitude_table(degrees, lon_count, False)
    inverse_table = longitude_table(degrees, lon_count, True)

    everyone = ("lat", "chan")
    sent = forward_transform(grid, scale, pair_list, table, owners, slots)
    by_degree = []
    returned = []
    for part, chunk in zip(sent, CHUNKS):
        count = chunk[1] - chunk[0]
        coefficients = analysis(exchange(part, "lat"), legendre_basis, firsts, chunk)
        filtered, kept = spectral_filter(exchange(coefficients, everyone), weights, count)
        by_degree.append(kept)
        lines = synthesize(
            exchange(filtered, everyone), legendre_basis, firsts, chunk, owners, lat_rows
        )
        returned.append(exchange(lines, "lat"))
    block_out, *grads = middle_transform(
        returned, grid, cotangent, pair_list, inverse_table, owners, slots
    )
    received = []
    for part, chunk in zip(grads, CHUNKS):
        coefficients = analysis(exchange(part, "lat"), legendre_basis, firsts, chunk)
        received.append(exchange(coefficients, everyone))
    counts = tuple(high - low for low, high in CHUNKS)
    weight_grad = exchange(filter_grad(received, by_degree, counts), "chan")
    weight_grad = weight_grad.swapaxes(0, 1).reshape(degrees_here, chan_rows, -1).astype(F32)
    return (block_out[None], weight_grad)


def solution(mesh):
    in_specs = (
        P(None, "lat", "chan", None),
        P("lat"),
        P("lat", None, None),
        P(),
        P(None, "chan", None),
        P(None, "lat", "chan", None),
    )
    out_specs = (P(None, "lat", "chan", None), P("lat", "chan", None))
    return jax.shard_map(
        on_device, mesh=mesh, in_specs=in_specs, out_specs=out_specs, check_vma=False
    )
```

```python
import functools
import math

import jax
import jax.numpy as jnp
import numpy as np
from jax import lax
from jax.experimental import pallas as pl
from jax.experimental.pallas import tpu as pltpu
from jax.sharding import PartitionSpec as P

F32 = jnp.float32
BF16 = jnp.bfloat16
GROUP = 32
T_STEP = 16
T_PART = 8
S_STEP = 4


def params(mib=56):
    return pltpu.CompilerParams(vmem_limit_bytes=mib << 20)


def cost(microseconds):
    return pl.CostEstimate(
        flops=int(microseconds * 1e9), bytes_accessed=1 << 20, transcendentals=0
    )


def round_up(value, unit):
    return -(-value // unit) * unit


def longitude_table(degrees, lon_count, doubled):
    first = np.arange(degrees // 2)
    orders = np.stack([first, degrees - 1 - first])
    phases = orders[:, :, None] * np.arange(lon_count) % lon_count
    angles = phases * (2.0 * math.pi / lon_count)
    table = np.stack([np.cos(angles), -np.sin(angles)], axis=1) / math.sqrt(lon_count)
    if doubled:
        table = table * np.where(orders == 0, 1.0, 2.0)[:, None, :, None]
    return jnp.asarray(table.reshape(2 * degrees, lon_count).astype(np.float32)).astype(BF16)


def swap_groups(tiles):
    lane = lax.broadcasted_iota(jnp.int32, tiles[0].shape, 1)
    low, even = lane < 64, lane // GROUP % 2 == 0
    t0, t1, t2, t3 = tiles
    a0 = jnp.where(low, t0, pltpu.roll(t2, 64, 1))
    a1 = jnp.where(low, t1, pltpu.roll(t3, 64, 1))
    a2 = jnp.where(low, pltpu.roll(t0, 64, 1), t2)
    a3 = jnp.where(low, pltpu.roll(t1, 64, 1), t3)
    return [
        jnp.where(even, a0, pltpu.roll(a1, 32, 1)),
        jnp.where(even, pltpu.roll(a0, 96, 1), a1),
        jnp.where(even, a2, pltpu.roll(a3, 32, 1)),
        jnp.where(even, pltpu.roll(a2, 96, 1), a3),
    ]


P_BLOCK = 32
PAD = 1


def by_latitude(rows_ref, stacked_ref, pairs, part, weight_of):
    for start in range(0, pairs, P_BLOCK):
        for q in range(T_PART // 4):
            lanes = slice(128 * q, 128 * q + 128)
            tiles = [
                rows_ref[part, wi * pairs + start : wi * pairs + start + P_BLOCK, lanes]
                for wi in range(4)
            ]
            for s, tile in enumerate(swap_groups(tiles)):
                t = part * T_PART + 4 * q + s
                row = t * (pairs + PAD) + start
                stacked_ref[row : row + P_BLOCK, :] = tile if weight_of is None else tile * weight_of[t]


def by_order(stacked_ref, rows_ref, pairs, q):
    for start in range(0, pairs, P_BLOCK):
        tiles = []
        for s in range(4):
            row = (4 * q + s) * (pairs + PAD) + start
            tiles.append(stacked_ref[row : row + P_BLOCK, :])
        for wi, tile in enumerate(swap_groups(tiles)):
            row = wi * pairs + start
            rows_ref[row : row + P_BLOCK, 128 * q : 128 * q + 128] = tile.astype(BF16)


def send_slots(pair_ref, stacked_ref, out_ref, pairs, slots):
    def step(owner, _):
        for k in range(slots):
            order = pair_ref[owner * slots + k]
            tile = stacked_ref[pl.ds(order, T_STEP, stride=pairs + PAD), :]
            out_ref[owner, k] = tile.astype(BF16)
        return 0

    lax.fori_loop(0, pairs // slots, step, 0)


def nt_dot(a, b):
    return lax.dot_general(a, b, (((1,), (1,)), ((), ())), preferred_element_type=F32)


def tn_dot(a, b):
    return lax.dot_general(a, b, (((0,), (0,)), ((), ())), preferred_element_type=F32)


def forward_body(pairs, slots, lat_rows, pair_ref, weight_ref, grid_ref, table_ref, out_ref, *refs):
    rows_ref, stacked_ref = refs
    start = pl.program_id(0) * T_STEP
    weight_of = [weight_ref[jnp.minimum(start + t, lat_rows - 1)] for t in range(T_STEP)]
    for part in range(T_STEP // T_PART):
        fields = grid_ref[part * T_PART : (part + 1) * T_PART].reshape(T_PART * GROUP, -1)
        rows_ref[part] = nt_dot(table_ref[...], fields)
        by_latitude(rows_ref, stacked_ref, pairs, part, weight_of)
    send_slots(pair_ref, stacked_ref, out_ref, pairs, slots)


def slot_spec(owners, slots):
    return pl.BlockSpec((owners, slots, T_STEP, 128), lambda t: (0, 0, t, 0))


def turn_scratch(pairs):
    return [
        pltpu.VMEM((T_STEP // T_PART, 4 * pairs, T_PART * GROUP), F32),
        pltpu.VMEM((T_STEP * (pairs + PAD), 128), F32),
    ]


def forward_transform(grid, weights, pair_list, table, owners, slots):
    lat_rows, _, lon_count = grid.shape
    pairs = owners * slots
    return pl.pallas_call(
        functools.partial(forward_body, pairs, slots, lat_rows),
        grid=(pl.cdiv(lat_rows, T_STEP),),
        in_specs=[
            pl.BlockSpec(memory_space=pltpu.SMEM),
            pl.BlockSpec(memory_space=pltpu.SMEM),
            pl.BlockSpec((T_STEP, GROUP, lon_count), lambda t: (t, 0, 0)),
            pl.BlockSpec((4 * pairs, lon_count), lambda t: (0, 0)),
        ],
        out_specs=slot_spec(owners, slots),
        out_shape=jax.ShapeDtypeStruct((owners, slots, lat_rows, 128), BF16),
        scratch_shapes=turn_scratch(pairs),
        compiler_params=params(),
        cost_estimate=cost(12),
        name="forward_transform",
    )(pair_list, weights, grid, table)


def middle_body(pairs, slots, pair_ref, in_ref, grid_ref, cot_ref, table_ref, *refs):
    field_ref, out_ref, rows_ref, stacked_ref, lines_ref, grad_ref = refs

    def step(owner, _):
        for k in range(slots):
            order = pair_ref[owner * slots + k]
            tile = in_ref[owner, k].astype(F32)
            stacked_ref[pl.ds(order, T_STEP, stride=pairs + PAD), :] = tile
        return 0

    lax.fori_loop(0, pairs // slots, step, 0)
    root = math.sqrt(2.0 / math.pi)
    for q in range(T_STEP // 4):
        by_order(stacked_ref, lines_ref, pairs, q)
        rows = slice(128 * q, 128 * q + 128)
        lats = slice(4 * q, 4 * q + 4)
        x = tn_dot(lines_ref[:, rows], table_ref[...])
        square = x * x
        th = jnp.tanh(x * (root + (root * 0.044715) * square))
        half = 0.5 + 0.5 * th
        gate = x * half
        slope = half + gate * (1.0 - th) * (root + (3.0 * root * 0.044715) * square)
        grid = grid_ref[lats].reshape(128, -1).astype(F32)
        field_ref[lats] = (grid + gate).astype(BF16).reshape(4, GROUP, -1)
        cot = cot_ref[lats].reshape(128, -1).astype(F32)
        grad_ref[rows, :] = (cot * slope).astype(BF16)
    for part in range(T_STEP // T_PART):
        grads = grad_ref[part * T_PART * GROUP : (part + 1) * T_PART * GROUP, :]
        rows_ref[part] = nt_dot(table_ref[...], grads)
        by_latitude(rows_ref, stacked_ref, pairs, part, None)
    send_slots(pair_ref, stacked_ref, out_ref, pairs, slots)


def middle_transform(returned, grid, cotangent, pair_list, table, owners, slots):
    lat_rows, _, lon_count = grid.shape
    pairs = owners * slots
    field_spec = pl.BlockSpec((T_STEP, GROUP, lon_count), lambda t: (t, 0, 0))
    return pl.pallas_call(
        functools.partial(middle_body, pairs, slots),
        grid=(pl.cdiv(lat_rows, T_STEP),),
        in_specs=[
            pl.BlockSpec(memory_space=pltpu.SMEM),
            slot_spec(owners, slots),
            field_spec,
            field_spec,
            pl.BlockSpec((4 * pairs, lon_count), lambda t: (0, 0)),
        ],
        out_specs=[field_spec, slot_spec(owners, slots)],
        out_shape=[
            jax.ShapeDtypeStruct(grid.shape, BF16),
            jax.ShapeDtypeStruct((owners, slots, lat_rows, 128), BF16),
        ],
        scratch_shapes=turn_scratch(pairs)
        + [
            pltpu.VMEM((4 * pairs, T_STEP * GROUP), BF16),
            pltpu.VMEM((T_STEP * GROUP, lon_count), BF16),
        ],
        compiler_params=params(),
        cost_estimate=cost(25),
        name="middle_transform",
    )(pair_list, returned, grid, cotangent, table)


def owned_tiles(degrees, chans, owners):
    return [divmod(tile, degrees // chans // owners) for tile in range(degrees // chans)]


def analysis_body(spread, firsts_ref, in_ref, basis_ref, out_ref, lats_ref, rows_ref, *refs):
    step = pl.program_id(0)
    owners, steps, lat_rows, _ = in_ref.shape
    degrees = basis_ref.shape[1] - 1
    degree = lax.broadcasted_iota(jnp.int32, (degrees, 128), 0)
    is_first = lax.broadcasted_iota(jnp.int32, (degrees, 128), 1) < 64

    if spread:
        sent_ref = refs[0]

        @pl.when(step == 0)
        def _():
            sent_ref[...] = jnp.zeros_like(sent_ref)

    for k in range(steps):
        for owner in range(owners):
            lats_ref[k, owner * lat_rows : (owner + 1) * lat_rows, :] = in_ref[owner, k].astype(F32)
        rows_ref[k, degrees + 1 :, :] = jnp.zeros((7, 128), F32)
    for k in range(steps):
        spectrum = lats_ref[k].astype(BF16)
        rows_ref[k, : degrees + 1, :] = jnp.dot(
            basis_ref[k], spectrum, preferred_element_type=F32
        )
    for k in range(steps):
        slot = step * steps + k
        first = firsts_ref[slot]
        leading = pltpu.roll(rows_ref[k], first, 0)[:degrees]
        trailing = rows_ref[k, 1 : degrees + 1, :]
        smallest = jnp.where(is_first, first, degrees - 1 - first)
        table = jnp.where(degree >= smallest, jnp.where(is_first, leading, trailing), 0.0)
        if spread:
            block_rows = out_ref.shape[1]
            for tile, (i, s) in enumerate(owned_tiles(degrees, 8, owners)):
                row = 8 * i * block_rows + 3 * slot + s
                sent_ref[pl.ds(row, 8, stride=block_rows), :] = table[8 * tile : 8 * tile + 8]
        else:
            part = degrees // owners
            for owner in range(owners):
                out_ref[owner, k] = table[part * owner : part * (owner + 1)].astype(BF16)

    if spread:

        @pl.when(step == pl.num_programs(0) - 1)
        def _():
            out_ref[...] = sent_ref[...].astype(BF16).reshape(out_ref.shape)


def analysis(arrived, basis, firsts, spread):
    owners, slots, lat_rows, _ = arrived.shape
    _, rows, lat_total = basis.shape
    degrees = rows - 1
    scratch = [
        pltpu.VMEM((S_STEP, lat_total, 128), F32),
        pltpu.VMEM((S_STEP, degrees + 8, 128), F32),
    ]
    if spread:
        block_rows = round_up(3 * slots, 8)
        shape = (owners * 8, block_rows, 128)
        out_spec = pl.BlockSpec(shape, lambda k: (0, 0, 0))
        scratch.append(pltpu.VMEM((owners * 8 * block_rows, 128), F32))
    else:
        part = degrees // owners
        shape = (owners, slots, part, 128)
        out_spec = pl.BlockSpec((owners, S_STEP, part, 128), lambda k: (0, k, 0, 0))
    return pl.pallas_call(
        functools.partial(analysis_body, spread),
        grid=(slots // S_STEP,),
        in_specs=[
            pl.BlockSpec(memory_space=pltpu.SMEM),
            pl.BlockSpec((owners, S_STEP, lat_rows, 128), lambda k: (0, k, 0, 0)),
            pl.BlockSpec((S_STEP, rows, lat_total), lambda k: (k, 0, 0)),
        ],
        out_specs=out_spec,
        out_shape=jax.ShapeDtypeStruct(shape, BF16),
        scratch_shapes=scratch,
        compiler_params=params(),
        cost_estimate=cost(6),
        name="analysis",
    )(firsts, arrived, basis)


def synthesis_body(firsts_ref, in_ref, basis_ref, out_ref, held_ref, rows_ref, lats_ref):
    step = pl.program_id(0)
    owners, steps, lat_rows, _ = out_ref.shape
    degrees = basis_ref.shape[1] - 1
    block_rows = in_ref.shape[1]
    size = degrees + 8
    row = lax.broadcasted_iota(jnp.int32, (size, 128), 0)
    is_first = lax.broadcasted_iota(jnp.int32, (size, 128), 1) < 64

    @pl.when(step == 0)
    def _():
        held_ref[...] = in_ref[...].astype(F32).reshape(held_ref.shape)
        rows_ref[...] = jnp.zeros_like(rows_ref)

    for k in range(steps):
        slot = step * steps + k
        for tile, (i, s) in enumerate(owned_tiles(degrees, 8, owners)):
            start = 8 * i * block_rows + 3 * slot + s
            rows_ref[k, 8 * tile : 8 * tile + 8, :] = held_ref[pl.ds(start, 8, stride=block_rows), :]
    for k in range(steps):
        first = firsts_ref[step * steps + k]
        table = rows_ref[k]
        leading = pltpu.roll(table, lax.rem(size - first, size), 0)
        trailing = pltpu.roll(table, 1, 0)
        lines = jnp.where(
            row < degrees - first,
            jnp.where(is_first, leading, 0.0),
            jnp.where(is_first, 0.0, trailing),
        )
        lats_ref[k] = tn_dot(basis_ref[k], lines[: degrees + 1].astype(BF16))
    for k in range(steps):
        for owner in range(owners):
            out_ref[owner, k] = lats_ref[k, owner * lat_rows : (owner + 1) * lat_rows, :].astype(BF16)


def synthesize(filtered, basis, firsts, owners, lat_rows):
    slots, rows, lat_total = basis.shape
    degrees = rows - 1
    devices, block_rows, _ = filtered.shape
    return pl.pallas_call(
        synthesis_body,
        grid=(slots // S_STEP,),
        in_specs=[
            pl.BlockSpec(memory_space=pltpu.SMEM),
            pl.BlockSpec((devices, block_rows, 128), lambda k: (0, 0, 0)),
            pl.BlockSpec((S_STEP, rows, lat_total), lambda k: (k, 0, 0)),
        ],
        out_specs=pl.BlockSpec((owners, S_STEP, lat_rows, 128), lambda k: (0, k, 0, 0)),
        out_shape=jax.ShapeDtypeStruct((owners, slots, lat_rows, 128), BF16),
        scratch_shapes=[
            pltpu.VMEM((devices * block_rows, 128), F32),
            pltpu.VMEM((S_STEP, degrees + 8, 128), F32),
            pltpu.VMEM((S_STEP, lat_total, 128), F32),
        ],
        compiler_params=params(),
        cost_estimate=cost(7),
        name="synthesis",
    )(firsts, filtered, basis)


HELD = 48
OWNER_UNROLL = 2


def filter_body(slots, me_ref, in_ref, weight_ref, out_ref, degree_ref, rows_ref, kept_ref, tight_ref):
    devices, block_rows, _ = in_ref.shape
    owners = devices // 8

    def gather(owner, _):
        start = pl.multiple_of(owner * HELD, 8)
        for half in range(2):
            lanes = slice(128 * half, 128 * half + 128)
            tiles = [in_ref[owner * 8 + 4 * half + a].astype(F32) for a in range(4)]
            for hj, tile in enumerate(swap_groups(tiles)):
                rows_ref[hj, half, pl.ds(start, block_rows), :] = tile
                rows_ref[hj, half, pl.ds(start + block_rows, HELD - block_rows), :] = jnp.zeros(
                    (HELD - block_rows, 128), F32
                )
        return 0

    lax.fori_loop(0, owners, gather, 0, unroll=OWNER_UNROLL)
    per_owner = HELD // 3
    for s in range(3):
        weights = weight_ref[:, s, 0].reshape(256, 256)
        for hj in range(4):
            table = [
                rows_ref[hj, half, pl.ds(s, owners * per_owner, stride=3), :] for half in range(2)
            ]
            for half in range(2):
                for i in range(owners):
                    row = (hj * owners + i) * slots
                    tight_ref[row : row + slots, 128 * half : 128 * half + 128] = table[half][
                        per_owner * i : per_owner * i + slots
                    ]
            whole = jnp.concatenate([half.astype(BF16) for half in table], axis=1)
            product = nt_dot(whole, weights)
            for half in range(2):
                kept_ref[hj, half, pl.ds(s, owners * per_owner, stride=3), :] = product[
                    :, 128 * half : 128 * half + 128
                ]
        degree_ref[s] = tight_ref[...].astype(BF16)

    def scatter(owner, _):
        start = pl.multiple_of(owner * HELD, 8)
        for half in range(2):
            tiles = [kept_ref[hj, half, pl.ds(start, block_rows), :] for hj in range(4)]
            for a, tile in enumerate(swap_groups(tiles)):
                out_ref[owner * 8 + 4 * half + a] = tile.astype(BF16)
        return 0

    lax.fori_loop(0, owners, scatter, 0, unroll=OWNER_UNROLL)


def spectral_filter(received, weights, me, slots):
    devices, block_rows, _ = received.shape
    owners = devices // 8
    whole = lambda shape: pl.BlockSpec(shape, lambda n, me_ref: (0,) * len(shape))
    degree_shape = (3, 4 * owners * slots, 256)
    return pl.pallas_call(
        functools.partial(filter_body, slots),
        grid_spec=pltpu.PrefetchScalarGridSpec(
            num_scalar_prefetch=1,
            grid=(1,),
            in_specs=[
                whole(received.shape),
                pl.BlockSpec((8, 3, 1, GROUP, 256), lambda n, me_ref: (0, 0, me_ref[0], 0, 0)),
            ],
            out_specs=[whole(received.shape), whole(degree_shape)],
            scratch_shapes=[
                pltpu.VMEM((4, 2, owners * HELD, 128), F32),
                pltpu.VMEM((4, 2, owners * HELD, 128), F32),
                pltpu.VMEM((4 * owners * slots, 256), F32),
            ],
        ),
        out_shape=[
            jax.ShapeDtypeStruct(received.shape, BF16),
            jax.ShapeDtypeStruct(degree_shape, BF16),
        ],
        compiler_params=params(),
        cost_estimate=cost(6),
        name="spectral_filter",
    )(me, received, weights)


def grad_body(in_ref, degree_ref, out_ref, rows_ref):
    step = pl.program_id(0)
    owners, slots, part, _ = in_ref.shape

    @pl.when(step == 0)
    def _():
        rows_ref[...] = in_ref[...].astype(F32).reshape(rows_ref.shape)

    group = lax.broadcasted_iota(jnp.int32, (owners * slots, 128), 1) // GROUP
    for j in range(8):
        grad = rows_ref[pl.ds(8 * step + j, owners * slots, stride=part), :]
        spread = [jnp.where(group == hj, grad, 0.0).astype(BF16) for hj in range(4)]
        sums = tn_dot(jnp.concatenate(spread, axis=0), degree_ref[j, 0])
        total = sums[:GROUP] + sums[GROUP : 2 * GROUP]
        out_ref[j] = total + (sums[2 * GROUP : 3 * GROUP] + sums[3 * GROUP :])


def filter_grad(received, by_degree):
    owners, slots, part, _ = received.shape
    chans, steps, rows, _ = by_degree.shape
    return pl.pallas_call(
        grad_body,
        grid=(steps,),
        in_specs=[
            pl.BlockSpec(received.shape, lambda s: (0, 0, 0, 0)),
            pl.BlockSpec((chans, 1, rows, 256), lambda s: (0, s, 0, 0)),
        ],
        out_specs=pl.BlockSpec((chans, GROUP, 256), lambda s: (s, 0, 0)),
        out_shape=jax.ShapeDtypeStruct((part, GROUP, 256), F32),
        scratch_shapes=[pltpu.VMEM((owners * slots * part, 128), F32)],
        compiler_params=params(),
        cost_estimate=cost(6),
        name="filter_grad",
    )(received, by_degree)


def exchange(array, axis):
    return lax.all_to_all(array, axis, split_axis=0, concat_axis=0, tiled=True)


def on_device(grid_in, lat_weights, legendre_basis, pair_list, filter_weights, cotangent):
    owners = lax.axis_size("lat")
    chans = lax.axis_size("chan")
    owner_index = lax.axis_index("lat")
    slots, rows, _ = legendre_basis.shape
    degrees = rows - 1
    _, lat_rows, chan_rows, lon_count = grid_in.shape
    grid, cotangent = grid_in[0], cotangent[0]
    firsts = lax.dynamic_slice_in_dim(pair_list, owner_index * slots, slots)
    me = lax.axis_index("chan").reshape(1).astype(jnp.int32)
    part = degrees // owners
    table = longitude_table(degrees, lon_count, False)
    inverse_table = longitude_table(degrees, lon_count, True)

    everyone = ("lat", "chan")
    spectrum = forward_transform(grid, lat_weights, pair_list, table, owners, slots)
    spectrum, filter_weights = lax.optimization_barrier((spectrum, filter_weights))
    weights = lax.dynamic_slice_in_dim(filter_weights, owner_index * part, part, 0)
    weights = lax.all_gather(weights, "chan")
    weights = weights.reshape(chans, part // chans, chans, chan_rows, -1)
    coefficients = analysis(exchange(spectrum, "lat"), legendre_basis, firsts, True)
    filtered, by_degree = spectral_filter(exchange(coefficients, everyone), weights, me, slots)
    filtered, by_degree = lax.optimization_barrier((exchange(filtered, everyone), by_degree))
    by_degree = lax.all_gather(by_degree, "chan")
    lines = synthesize(filtered, legendre_basis, firsts, owners, lat_rows)
    block_out, grads = middle_transform(
        exchange(lines, "lat"), grid, cotangent, pair_list, inverse_table, owners, slots
    )
    grads = analysis(exchange(grads, "lat"), legendre_basis, firsts, False)
    weight_grad = filter_grad(exchange(grads, "lat"), by_degree)
    return (block_out[None], weight_grad)


def solution(mesh):
    in_specs = (
        P(None, "lat", "chan", None),
        P("lat"),
        P("lat", None, None),
        P(),
        P(None, "chan", None),
        P(None, "lat", "chan", None),
    )
    out_specs = (P(None, "lat", "chan", None), P("lat", "chan", None))
    return jax.shard_map(
        on_device, mesh=mesh, in_specs=in_specs, out_specs=out_specs, check_vma=False
    )
```

```python
import functools
import math

import jax
import jax.numpy as jnp
import numpy as np
from jax import lax
from jax.experimental import pallas as pl
from jax.experimental.pallas import tpu as pltpu
from jax.sharding import PartitionSpec as P

F32 = jnp.float32
BF16 = jnp.bfloat16
GROUP = 32
T_STEP = 16
T_PART = 8
S_STEP = 4


def params(mib):
    return pltpu.CompilerParams(vmem_limit_bytes=mib << 20)


def cost(microseconds):
    return pl.CostEstimate(
        flops=int(microseconds * 1e9), bytes_accessed=1 << 20, transcendentals=0
    )


def round_up(value, unit):
    return -(-value // unit) * unit


def longitude_table(degrees, lon_count, doubled):
    first = np.arange(degrees // 2)
    orders = np.stack([first, degrees - 1 - first])
    phases = orders[:, :, None] * np.arange(lon_count) % lon_count
    angles = phases * (2.0 * math.pi / lon_count)
    table = np.stack([np.cos(angles), -np.sin(angles)], axis=1) / math.sqrt(lon_count)
    if doubled:
        table = table * np.where(orders == 0, 1.0, 2.0)[:, None, :, None]
    return jnp.asarray(table.reshape(2 * degrees, lon_count).astype(np.float32)).astype(BF16)


def swap_groups(tiles):
    lane = lax.broadcasted_iota(jnp.int32, tiles[0].shape, 1)
    low, even = lane < 64, lane // GROUP % 2 == 0
    t0, t1, t2, t3 = tiles
    a0 = jnp.where(low, t0, pltpu.roll(t2, 64, 1))
    a1 = jnp.where(low, t1, pltpu.roll(t3, 64, 1))
    a2 = jnp.where(low, pltpu.roll(t0, 64, 1), t2)
    a3 = jnp.where(low, pltpu.roll(t1, 64, 1), t3)
    return [
        jnp.where(even, a0, pltpu.roll(a1, 32, 1)),
        jnp.where(even, pltpu.roll(a0, 96, 1), a1),
        jnp.where(even, a2, pltpu.roll(a3, 32, 1)),
        jnp.where(even, pltpu.roll(a2, 96, 1), a3),
    ]


P_BLOCK = 32
PAD = 1


def by_latitude(rows_ref, stacked_ref, pairs, part, weight_of):
    for start in range(0, pairs, P_BLOCK):
        for q in range(T_PART // 4):
            lanes = slice(128 * q, 128 * q + 128)
            tiles = [
                rows_ref[part, wi * pairs + start : wi * pairs + start + P_BLOCK, lanes]
                for wi in range(4)
            ]
            for s, tile in enumerate(swap_groups(tiles)):
                t = part * T_PART + 4 * q + s
                row = t * (pairs + PAD) + start
                stacked_ref[row : row + P_BLOCK, :] = tile if weight_of is None else tile * weight_of[t]


def by_order(stacked_ref, rows_ref, pairs, q):
    for start in range(0, pairs, P_BLOCK):
        tiles = []
        for s in range(4):
            row = (4 * q + s) * (pairs + PAD) + start
            tiles.append(stacked_ref[row : row + P_BLOCK, :])
        for wi, tile in enumerate(swap_groups(tiles)):
            row = wi * pairs + start
            rows_ref[row : row + P_BLOCK, 128 * q : 128 * q + 128] = tile.astype(BF16)


def send_slots(pair_ref, stacked_ref, out_ref, pairs, slots):
    def step(owner, _):
        for k in range(slots):
            order = pair_ref[owner * slots + k]
            tile = stacked_ref[pl.ds(order, T_STEP, stride=pairs + PAD), :]
            out_ref[owner, k] = tile.astype(BF16)
        return 0

    lax.fori_loop(0, pairs // slots, step, 0)


def nt_dot(a, b):
    return lax.dot_general(a, b, (((1,), (1,)), ((), ())), preferred_element_type=F32)


def tn_dot(a, b):
    return lax.dot_general(a, b, (((0,), (0,)), ((), ())), preferred_element_type=F32)


def forward_body(pairs, slots, lat_rows, owner_ref, pair_ref, weight_ref, *refs):
    grid_ref, table_ref, filter_ref, out_ref, part_ref, rows_ref, stacked_ref = refs
    start = pl.program_id(0) * T_STEP

    @pl.when(start == 0)
    def _():
        part_ref[...] = filter_ref[...]

    weight_of = [weight_ref[jnp.minimum(start + t, lat_rows - 1)] for t in range(T_STEP)]
    for part in range(T_STEP // T_PART):
        fields = grid_ref[part * T_PART : (part + 1) * T_PART].reshape(T_PART * GROUP, -1)
        rows_ref[part] = nt_dot(table_ref[...], fields)
        by_latitude(rows_ref, stacked_ref, pairs, part, weight_of)
    send_slots(pair_ref, stacked_ref, out_ref, pairs, slots)


def slot_spec(owners, slots):
    return pl.BlockSpec((owners, slots, T_STEP, 128), lambda t: (0, 0, t, 0))


def turn_scratch(pairs):
    return [
        pltpu.VMEM((T_STEP // T_PART, 4 * pairs, T_PART * GROUP), F32),
        pltpu.VMEM((T_STEP * (pairs + PAD), 128), F32),
    ]


def forward_transform(grid, weights, pair_list, table, filters, owner, owners, slots):
    lat_rows, _, lon_count = grid.shape
    pairs = owners * slots
    part_shape = (filters.shape[0] // owners,) + filters.shape[1:]
    return pl.pallas_call(
        functools.partial(forward_body, pairs, slots, lat_rows),
        grid_spec=pltpu.PrefetchScalarGridSpec(
            num_scalar_prefetch=1,
            grid=(pl.cdiv(lat_rows, T_STEP),),
            in_specs=[
                pl.BlockSpec(memory_space=pltpu.SMEM),
                pl.BlockSpec(memory_space=pltpu.SMEM),
                pl.BlockSpec((T_STEP, GROUP, lon_count), lambda t, owner_ref: (t, 0, 0)),
                pl.BlockSpec((4 * pairs, lon_count), lambda t, owner_ref: (0, 0)),
                pl.BlockSpec(part_shape, lambda t, owner_ref: (owner_ref[0], 0, 0)),
            ],
            out_specs=[
                pl.BlockSpec((owners, slots, T_STEP, 128), lambda t, owner_ref: (0, 0, t, 0)),
                pl.BlockSpec(part_shape, lambda t, owner_ref: (0, 0, 0)),
            ],
            scratch_shapes=turn_scratch(pairs),
        ),
        out_shape=[
            jax.ShapeDtypeStruct((owners, slots, lat_rows, 128), BF16),
            jax.ShapeDtypeStruct(part_shape, BF16),
        ],
        compiler_params=params(56),
        cost_estimate=cost(12),
        name="forward_transform",
    )(owner, pair_list, weights, grid, table, filters)


def middle_body(pairs, slots, pair_ref, in_ref, cot_ref, table_ref, *refs):
    field_ref, out_ref, rows_ref, stacked_ref, lines_ref, grad_ref = refs

    def step(owner, _):
        for k in range(slots):
            order = pair_ref[owner * slots + k]
            tile = in_ref[owner, k].astype(F32)
            stacked_ref[pl.ds(order, T_STEP, stride=pairs + PAD), :] = tile
        return 0

    lax.fori_loop(0, pairs // slots, step, 0)
    root = math.sqrt(2.0 / math.pi)
    for q in range(T_STEP // 4):
        by_order(stacked_ref, lines_ref, pairs, q)
        rows = slice(128 * q, 128 * q + 128)
        lats = slice(4 * q, 4 * q + 4)
        x = tn_dot(lines_ref[:, rows], table_ref[...])
        square = x * x
        th = jnp.tanh(x * (root + (root * 0.044715) * square))
        half = 0.5 + 0.5 * th
        gate = x * half
        slope = half + gate * (1.0 - th) * (root + (3.0 * root * 0.044715) * square)
        field_ref[lats] = gate.astype(BF16).reshape(4, GROUP, -1)
        cot = cot_ref[lats].reshape(128, -1).astype(F32)
        grad_ref[rows, :] = (cot * slope).astype(BF16)
    for part in range(T_STEP // T_PART):
        grads = grad_ref[part * T_PART * GROUP : (part + 1) * T_PART * GROUP, :]
        rows_ref[part] = nt_dot(table_ref[...], grads)
        by_latitude(rows_ref, stacked_ref, pairs, part, None)
    send_slots(pair_ref, stacked_ref, out_ref, pairs, slots)


def middle_transform(returned, cotangent, pair_list, table, owners, slots):
    lat_rows, _, lon_count = cotangent.shape
    pairs = owners * slots
    field_spec = pl.BlockSpec((T_STEP, GROUP, lon_count), lambda t: (t, 0, 0))
    return pl.pallas_call(
        functools.partial(middle_body, pairs, slots),
        grid=(pl.cdiv(lat_rows, T_STEP),),
        in_specs=[
            pl.BlockSpec(memory_space=pltpu.SMEM),
            slot_spec(owners, slots),
            field_spec,
            pl.BlockSpec((4 * pairs, lon_count), lambda t: (0, 0)),
        ],
        out_specs=[field_spec, slot_spec(owners, slots)],
        out_shape=[
            jax.ShapeDtypeStruct(cotangent.shape, BF16),
            jax.ShapeDtypeStruct((owners, slots, lat_rows, 128), BF16),
        ],
        scratch_shapes=turn_scratch(pairs)
        + [
            pltpu.VMEM((4 * pairs, T_STEP * GROUP), BF16),
            pltpu.VMEM((T_STEP * GROUP, lon_count), BF16),
        ],
        compiler_params=params(46),
        cost_estimate=cost(25),
        name="middle_transform",
    )(pair_list, returned, cotangent, table)


def owned_tiles(degrees, chans, owners):
    return [divmod(tile, degrees // chans // owners) for tile in range(degrees // chans)]


def analysis_body(spread, owner_ref, pair_ref, in_ref, basis_ref, out_ref, lats_ref, rows_ref, *refs):
    step = pl.program_id(0)
    owners, steps, lat_rows, _ = in_ref.shape
    degrees = basis_ref.shape[1] - 1
    degree = lax.broadcasted_iota(jnp.int32, (degrees, 128), 0)
    is_first = lax.broadcasted_iota(jnp.int32, (degrees, 128), 1) < 64

    if spread:
        sent_ref = refs[0]

        @pl.when(step == 0)
        def _():
            sent_ref[...] = jnp.zeros_like(sent_ref)

    for k in range(steps):
        for owner in range(owners):
            lats_ref[k, owner * lat_rows : (owner + 1) * lat_rows, :] = in_ref[owner, k].astype(F32)
        rows_ref[k, degrees + 1 :, :] = jnp.zeros((7, 128), F32)
    for k in range(steps):
        spectrum = lats_ref[k].astype(BF16)
        rows_ref[k, : degrees + 1, :] = jnp.dot(
            basis_ref[k], spectrum, preferred_element_type=F32
        )
    for k in range(steps):
        slot = step * steps + k
        first = pair_ref[owner_ref[0] * pl.num_programs(0) * steps + slot]
        leading = pltpu.roll(rows_ref[k], first, 0)[:degrees]
        trailing = rows_ref[k, 1 : degrees + 1, :]
        smallest = jnp.where(is_first, first, degrees - 1 - first)
        table = jnp.where(degree >= smallest, jnp.where(is_first, leading, trailing), 0.0)
        if spread:
            block_rows = out_ref.shape[1]
            for tile, (i, s) in enumerate(owned_tiles(degrees, 8, owners)):
                row = 8 * i * block_rows + 3 * slot + s
                sent_ref[pl.ds(row, 8, stride=block_rows), :] = table[8 * tile : 8 * tile + 8]
        else:
            part = degrees // owners
            for owner in range(owners):
                out_ref[owner, k] = table[part * owner : part * (owner + 1)].astype(BF16)

    if spread:

        @pl.when(step == pl.num_programs(0) - 1)
        def _():
            out_ref[...] = sent_ref[...].astype(BF16).reshape(out_ref.shape)


def analysis(arrived, basis, places, spread):
    owners, slots, lat_rows, _ = arrived.shape
    _, rows, lat_total = basis.shape
    degrees = rows - 1
    scratch = [
        pltpu.VMEM((S_STEP, lat_total, 128), F32),
        pltpu.VMEM((S_STEP, degrees + 8, 128), F32),
    ]
    if spread:
        block_rows = round_up(3 * slots, 8)
        shape = (owners * 8, block_rows, 128)
        out_spec = pl.BlockSpec(shape, lambda k: (0, 0, 0))
        scratch.append(pltpu.VMEM((owners * 8 * block_rows, 128), F32))
    else:
        part = degrees // owners
        shape = (owners, slots, part, 128)
        out_spec = pl.BlockSpec((owners, S_STEP, part, 128), lambda k: (0, k, 0, 0))
    return pl.pallas_call(
        functools.partial(analysis_body, spread),
        grid=(slots // S_STEP,),
        in_specs=[
            pl.BlockSpec(memory_space=pltpu.SMEM),
            pl.BlockSpec(memory_space=pltpu.SMEM),
            pl.BlockSpec((owners, S_STEP, lat_rows, 128), lambda k: (0, k, 0, 0)),
            pl.BlockSpec((S_STEP, rows, lat_total), lambda k: (k, 0, 0)),
        ],
        out_specs=out_spec,
        out_shape=jax.ShapeDtypeStruct(shape, BF16),
        scratch_shapes=scratch,
        compiler_params=params(18),
        cost_estimate=cost(6),
        name="analysis",
    )(*places, arrived, basis)


def synthesis_body(owner_ref, pair_ref, in_ref, basis_ref, out_ref, held_ref, rows_ref, lats_ref):
    step = pl.program_id(0)
    owners, steps, lat_rows, _ = out_ref.shape
    degrees = basis_ref.shape[1] - 1
    block_rows = in_ref.shape[1]
    size = degrees + 8
    row = lax.broadcasted_iota(jnp.int32, (size, 128), 0)
    is_first = lax.broadcasted_iota(jnp.int32, (size, 128), 1) < 64

    @pl.when(step == 0)
    def _():
        held_ref[...] = in_ref[...].astype(F32).reshape(held_ref.shape)
        rows_ref[...] = jnp.zeros_like(rows_ref)

    for k in range(steps):
        slot = step * steps + k
        for tile, (i, s) in enumerate(owned_tiles(degrees, 8, owners)):
            start = 8 * i * block_rows + 3 * slot + s
            rows_ref[k, 8 * tile : 8 * tile + 8, :] = held_ref[pl.ds(start, 8, stride=block_rows), :]
    for k in range(steps):
        first = pair_ref[(owner_ref[0] * pl.num_programs(0) + step) * steps + k]
        table = rows_ref[k]
        leading = pltpu.roll(table, lax.rem(size - first, size), 0)
        trailing = pltpu.roll(table, 1, 0)
        lines = jnp.where(
            row < degrees - first,
            jnp.where(is_first, leading, 0.0),
            jnp.where(is_first, 0.0, trailing),
        )
        lats_ref[k] = tn_dot(basis_ref[k], lines[: degrees + 1].astype(BF16))
    for k in range(steps):
        for owner in range(owners):
            out_ref[owner, k] = lats_ref[k, owner * lat_rows : (owner + 1) * lat_rows, :].astype(BF16)


def synthesize(filtered, basis, places, owners, lat_rows):
    slots, rows, lat_total = basis.shape
    degrees = rows - 1
    devices, block_rows, _ = filtered.shape
    return pl.pallas_call(
        synthesis_body,
        grid=(slots // S_STEP,),
        in_specs=[
            pl.BlockSpec(memory_space=pltpu.SMEM),
            pl.BlockSpec(memory_space=pltpu.SMEM),
            pl.BlockSpec((devices, block_rows, 128), lambda k: (0, 0, 0)),
            pl.BlockSpec((S_STEP, rows, lat_total), lambda k: (k, 0, 0)),
        ],
        out_specs=pl.BlockSpec((owners, S_STEP, lat_rows, 128), lambda k: (0, k, 0, 0)),
        out_shape=jax.ShapeDtypeStruct((owners, slots, lat_rows, 128), BF16),
        scratch_shapes=[
            pltpu.VMEM((devices * block_rows, 128), F32),
            pltpu.VMEM((S_STEP, degrees + 8, 128), F32),
            pltpu.VMEM((S_STEP, lat_total, 128), F32),
        ],
        compiler_params=params(18),
        cost_estimate=cost(7),
        name="synthesis",
    )(*places, filtered, basis)


HELD = 48
OWNER_UNROLL = 2


def filter_body(slots, me_ref, in_ref, weight_ref, out_ref, degree_ref, rows_ref, kept_ref, tight_ref):
    devices, block_rows, _ = in_ref.shape
    owners = devices // 8

    def gather(owner, _):
        start = pl.multiple_of(owner * HELD, 8)
        for half in range(2):
            lanes = slice(128 * half, 128 * half + 128)
            tiles = [in_ref[owner * 8 + 4 * half + a].astype(F32) for a in range(4)]
            for hj, tile in enumerate(swap_groups(tiles)):
                rows_ref[hj, half, pl.ds(start, block_rows), :] = tile
                rows_ref[hj, half, pl.ds(start + block_rows, HELD - block_rows), :] = jnp.zeros(
                    (HELD - block_rows, 128), F32
                )
        return 0

    lax.fori_loop(0, owners, gather, 0, unroll=OWNER_UNROLL)
    per_owner = HELD // 3
    for s in range(3):
        weights = weight_ref[:, s, 0].reshape(256, 256)
        for hj in range(4):
            table = [
                rows_ref[hj, half, pl.ds(s, owners * per_owner, stride=3), :] for half in range(2)
            ]
            for half in range(2):
                for i in range(owners):
                    row = (hj * owners + i) * slots
                    tight_ref[row : row + slots, 128 * half : 128 * half + 128] = table[half][
                        per_owner * i : per_owner * i + slots
                    ]
            whole = jnp.concatenate([half.astype(BF16) for half in table], axis=1)
            product = nt_dot(whole, weights)
            for half in range(2):
                kept_ref[hj, half, pl.ds(s, owners * per_owner, stride=3), :] = product[
                    :, 128 * half : 128 * half + 128
                ]
        degree_ref[s] = tight_ref[...].astype(BF16)

    def scatter(owner, _):
        start = pl.multiple_of(owner * HELD, 8)
        for half in range(2):
            tiles = [kept_ref[hj, half, pl.ds(start, block_rows), :] for hj in range(4)]
            for a, tile in enumerate(swap_groups(tiles)):
                out_ref[owner * 8 + 4 * half + a] = tile.astype(BF16)
        return 0

    lax.fori_loop(0, owners, scatter, 0, unroll=OWNER_UNROLL)


def spectral_filter(received, weights, me, slots):
    devices, block_rows, _ = received.shape
    owners = devices // 8
    whole = lambda shape: pl.BlockSpec(shape, lambda n, me_ref: (0,) * len(shape))
    degree_shape = (3, 4 * owners * slots, 256)
    return pl.pallas_call(
        functools.partial(filter_body, slots),
        grid_spec=pltpu.PrefetchScalarGridSpec(
            num_scalar_prefetch=1,
            grid=(1,),
            in_specs=[
                whole(received.shape),
                pl.BlockSpec((8, 3, 1, GROUP, 256), lambda n, me_ref: (0, 0, me_ref[0], 0, 0)),
            ],
            out_specs=[whole(received.shape), whole(degree_shape)],
            scratch_shapes=[
                pltpu.VMEM((4, 2, owners * HELD, 128), F32),
                pltpu.VMEM((4, 2, owners * HELD, 128), F32),
                pltpu.VMEM((4 * owners * slots, 256), F32),
            ],
        ),
        out_shape=[
            jax.ShapeDtypeStruct(received.shape, BF16),
            jax.ShapeDtypeStruct(degree_shape, BF16),
        ],
        compiler_params=params(22),
        cost_estimate=cost(6),
        name="spectral_filter",
    )(me, received, weights)


def grad_body(in_ref, degree_ref, out_ref, rows_ref):
    step = pl.program_id(0)
    owners, slots, part, _ = in_ref.shape

    @pl.when(step == 0)
    def _():
        rows_ref[...] = in_ref[...].astype(F32).reshape(rows_ref.shape)

    group = lax.broadcasted_iota(jnp.int32, (owners * slots, 128), 1) // GROUP
    for j in range(8):
        grad = rows_ref[pl.ds(8 * step + j, owners * slots, stride=part), :]
        spread = [jnp.where(group == hj, grad, 0.0).astype(BF16) for hj in range(4)]
        sums = tn_dot(jnp.concatenate(spread, axis=0), degree_ref[j, 0])
        total = sums[:GROUP] + sums[GROUP : 2 * GROUP]
        out_ref[j] = total + (sums[2 * GROUP : 3 * GROUP] + sums[3 * GROUP :])


def filter_grad(received, by_degree):
    owners, slots, part, _ = received.shape
    chans, steps, rows, _ = by_degree.shape
    return pl.pallas_call(
        grad_body,
        grid=(steps,),
        in_specs=[
            pl.BlockSpec(received.shape, lambda s: (0, 0, 0, 0)),
            pl.BlockSpec((chans, 1, rows, 256), lambda s: (0, s, 0, 0)),
        ],
        out_specs=pl.BlockSpec((chans, GROUP, 256), lambda s: (s, 0, 0)),
        out_shape=jax.ShapeDtypeStruct((part, GROUP, 256), F32),
        scratch_shapes=[pltpu.VMEM((owners * slots * part, 128), F32)],
        compiler_params=params(40),
        cost_estimate=cost(6),
        name="filter_grad",
    )(received, by_degree)


def exchange(array, axis):
    return lax.all_to_all(array, axis, split_axis=0, concat_axis=0, tiled=True)


def on_device(grid_in, lat_weights, legendre_basis, pair_list, filter_weights, cotangent):
    owners = lax.axis_size("lat")
    chans = lax.axis_size("chan")
    slots, rows, _ = legendre_basis.shape
    degrees = rows - 1
    _, lat_rows, chan_rows, lon_count = grid_in.shape
    grid, cotangent = grid_in[0], cotangent[0]
    owner = lax.axis_index("lat").reshape(1).astype(jnp.int32)
    me = lax.axis_index("chan").reshape(1).astype(jnp.int32)
    places = (owner, pair_list)
    table = longitude_table(degrees, lon_count, False)
    inverse_table = longitude_table(degrees, lon_count, True)

    everyone = ("lat", "chan")
    spectrum, weights = forward_transform(
        grid, lat_weights, pair_list, table, filter_weights, owner, owners, slots
    )
    weights = lax.all_gather(weights, "chan")
    weights = weights.reshape(chans, degrees // owners // chans, chans, chan_rows, -1)
    coefficients = analysis(exchange(spectrum, "lat"), legendre_basis, places, True)
    filtered, by_degree = spectral_filter(exchange(coefficients, everyone), weights, me, slots)
    filtered, by_degree = lax.optimization_barrier((exchange(filtered, everyone), by_degree))
    by_degree = lax.all_gather(by_degree, "chan")
    lines = synthesize(filtered, legendre_basis, places, owners, lat_rows)
    gate, grads = middle_transform(
        exchange(lines, "lat"), cotangent, pair_list, inverse_table, owners, slots
    )
    grads = analysis(exchange(grads, "lat"), legendre_basis, places, False)
    weight_grad = filter_grad(exchange(grads, "lat"), by_degree)
    block_out = (grid.astype(F32) + gate.astype(F32)).astype(BF16)
    return (block_out[None], weight_grad)


def solution(mesh):
    in_specs = (
        P(None, "lat", "chan", None),
        P("lat"),
        P("lat", None, None),
        P(),
        P(None, "chan", None),
        P(None, "lat", "chan", None),
    )
    out_specs = (P(None, "lat", "chan", None), P("lat", "chan", None))
    return jax.shard_map(
        on_device, mesh=mesh, in_specs=in_specs, out_specs=out_specs, check_vma=False
    )
```

```python
import functools
import math

import jax
import jax.numpy as jnp
import numpy as np
from jax import lax
from jax.experimental import pallas as pl
from jax.experimental.pallas import tpu as pltpu
from jax.sharding import PartitionSpec as P

F32 = jnp.float32
BF16 = jnp.bfloat16
GROUP = 32
T_STEP = 16
T_PART = 8
S_STEP = 6


def params(mib):
    return pltpu.CompilerParams(vmem_limit_bytes=mib << 20)


def cost(microseconds):
    return pl.CostEstimate(
        flops=int(microseconds * 1e9), bytes_accessed=1 << 20, transcendentals=0
    )


def round_up(value, unit):
    return -(-value // unit) * unit


def longitude_table(degrees, lon_count, doubled):
    first = np.arange(degrees // 2)
    orders = np.stack([first, degrees - 1 - first])
    phases = orders[:, :, None] * np.arange(lon_count) % lon_count
    angles = phases * (2.0 * math.pi / lon_count)
    table = np.stack([np.cos(angles), -np.sin(angles)], axis=1) / math.sqrt(lon_count)
    if doubled:
        table = table * np.where(orders == 0, 1.0, 2.0)[:, None, :, None]
    return jnp.asarray(table.reshape(2 * degrees, lon_count).astype(np.float32)).astype(BF16)


def swap_groups(tiles):
    lane = lax.broadcasted_iota(jnp.int32, tiles[0].shape, 1)
    low, even = lane < 64, lane // GROUP % 2 == 0
    t0, t1, t2, t3 = tiles
    a0 = jnp.where(low, t0, pltpu.roll(t2, 64, 1))
    a1 = jnp.where(low, t1, pltpu.roll(t3, 64, 1))
    a2 = jnp.where(low, pltpu.roll(t0, 64, 1), t2)
    a3 = jnp.where(low, pltpu.roll(t1, 64, 1), t3)
    return [
        jnp.where(even, a0, pltpu.roll(a1, 32, 1)),
        jnp.where(even, pltpu.roll(a0, 96, 1), a1),
        jnp.where(even, a2, pltpu.roll(a3, 32, 1)),
        jnp.where(even, pltpu.roll(a2, 96, 1), a3),
    ]


P_BLOCK = 32
PAD = 1


def by_latitude(rows_ref, stacked_ref, pairs, part, weight_of):
    for start in range(0, pairs, P_BLOCK):
        for q in range(T_PART // 4):
            lanes = slice(128 * q, 128 * q + 128)
            tiles = [
                rows_ref[part, wi * pairs + start : wi * pairs + start + P_BLOCK, lanes]
                for wi in range(4)
            ]
            for s, tile in enumerate(swap_groups(tiles)):
                t = part * T_PART + 4 * q + s
                row = t * (pairs + PAD) + start
                stacked_ref[row : row + P_BLOCK, :] = tile if weight_of is None else tile * weight_of[t]


def by_order(stacked_ref, rows_ref, pairs, q):
    for start in range(0, pairs, P_BLOCK):
        tiles = []
        for s in range(4):
            row = (4 * q + s) * (pairs + PAD) + start
            tiles.append(stacked_ref[row : row + P_BLOCK, :])
        for wi, tile in enumerate(swap_groups(tiles)):
            row = wi * pairs + start
            rows_ref[row : row + P_BLOCK, 128 * q : 128 * q + 128] = tile.astype(BF16)


def send_slots(pair_ref, stacked_ref, out_ref, pairs, slots):
    def step(owner, _):
        for k in range(slots):
            order = pair_ref[owner * slots + k]
            tile = stacked_ref[pl.ds(order, T_STEP, stride=pairs + PAD), :]
            out_ref[owner, k] = tile.astype(BF16)
        return 0

    lax.fori_loop(0, pairs // slots, step, 0)


def nt_dot(a, b):
    return lax.dot_general(a, b, (((1,), (1,)), ((), ())), preferred_element_type=F32)


def tn_dot(a, b):
    return lax.dot_general(a, b, (((0,), (0,)), ((), ())), preferred_element_type=F32)


def forward_body(pairs, slots, lat_rows, owner_ref, pair_ref, weight_ref, *refs):
    grid_ref, table_ref, filter_ref, out_ref, part_ref, rows_ref, stacked_ref = refs
    start = pl.program_id(0) * T_STEP

    @pl.when(start == 0)
    def _():
        part_ref[...] = filter_ref[...]

    weight_of = [weight_ref[jnp.minimum(start + t, lat_rows - 1)] for t in range(T_STEP)]
    for part in range(T_STEP // T_PART):
        fields = grid_ref[part * T_PART : (part + 1) * T_PART].reshape(T_PART * GROUP, -1)
        rows_ref[part] = nt_dot(table_ref[...], fields)
        by_latitude(rows_ref, stacked_ref, pairs, part, weight_of)
    send_slots(pair_ref, stacked_ref, out_ref, pairs, slots)


def slot_spec(owners, slots):
    return pl.BlockSpec((owners, slots, T_STEP, 128), lambda t: (0, 0, t, 0))


def turn_scratch(pairs):
    return [
        pltpu.VMEM((T_STEP // T_PART, 4 * pairs, T_PART * GROUP), F32),
        pltpu.VMEM((T_STEP * (pairs + PAD), 128), F32),
    ]


def forward_transform(grid, weights, pair_list, table, filters, owner, owners, slots):
    lat_rows, _, lon_count = grid.shape
    pairs = owners * slots
    part_shape = (filters.shape[0] // owners,) + filters.shape[1:]
    return pl.pallas_call(
        functools.partial(forward_body, pairs, slots, lat_rows),
        grid_spec=pltpu.PrefetchScalarGridSpec(
            num_scalar_prefetch=1,
            grid=(pl.cdiv(lat_rows, T_STEP),),
            in_specs=[
                pl.BlockSpec(memory_space=pltpu.SMEM),
                pl.BlockSpec(memory_space=pltpu.SMEM),
                pl.BlockSpec((T_STEP, GROUP, lon_count), lambda t, owner_ref: (t, 0, 0)),
                pl.BlockSpec((4 * pairs, lon_count), lambda t, owner_ref: (0, 0)),
                pl.BlockSpec(part_shape, lambda t, owner_ref: (owner_ref[0], 0, 0)),
            ],
            out_specs=[
                pl.BlockSpec((owners, slots, T_STEP, 128), lambda t, owner_ref: (0, 0, t, 0)),
                pl.BlockSpec(part_shape, lambda t, owner_ref: (0, 0, 0)),
            ],
            scratch_shapes=turn_scratch(pairs),
        ),
        out_shape=[
            jax.ShapeDtypeStruct((owners, slots, lat_rows, 128), BF16),
            jax.ShapeDtypeStruct(part_shape, BF16),
        ],
        compiler_params=params(56),
        cost_estimate=cost(12),
        name="forward_transform",
    )(owner, pair_list, weights, grid, table, filters)


def middle_body(pairs, slots, pair_ref, in_ref, cot_ref, table_ref, *refs):
    field_ref, out_ref, rows_ref, stacked_ref, lines_ref, grad_ref = refs

    def step(owner, _):
        for k in range(slots):
            order = pair_ref[owner * slots + k]
            tile = in_ref[owner, k].astype(F32)
            stacked_ref[pl.ds(order, T_STEP, stride=pairs + PAD), :] = tile
        return 0

    lax.fori_loop(0, pairs // slots, step, 0)
    root = math.sqrt(2.0 / math.pi)
    for q in range(T_STEP // 4):
        by_order(stacked_ref, lines_ref, pairs, q)
        rows = slice(128 * q, 128 * q + 128)
        lats = slice(4 * q, 4 * q + 4)
        x = tn_dot(lines_ref[:, rows], table_ref[...])
        square = x * x
        th = jnp.tanh(x * (root + (root * 0.044715) * square))
        half = 0.5 + 0.5 * th
        gate = x * half
        slope = half + gate * (1.0 - th) * (root + (3.0 * root * 0.044715) * square)
        field_ref[lats] = gate.astype(BF16).reshape(4, GROUP, -1)
        cot = cot_ref[lats].reshape(128, -1).astype(F32)
        grad_ref[rows, :] = (cot * slope).astype(BF16)
    for part in range(T_STEP // T_PART):
        grads = grad_ref[part * T_PART * GROUP : (part + 1) * T_PART * GROUP, :]
        rows_ref[part] = nt_dot(table_ref[...], grads)
        by_latitude(rows_ref, stacked_ref, pairs, part, None)
    send_slots(pair_ref, stacked_ref, out_ref, pairs, slots)


def middle_transform(returned, cotangent, pair_list, table, owners, slots):
    lat_rows, _, lon_count = cotangent.shape
    pairs = owners * slots
    field_spec = pl.BlockSpec((T_STEP, GROUP, lon_count), lambda t: (t, 0, 0))
    return pl.pallas_call(
        functools.partial(middle_body, pairs, slots),
        grid=(pl.cdiv(lat_rows, T_STEP),),
        in_specs=[
            pl.BlockSpec(memory_space=pltpu.SMEM),
            slot_spec(owners, slots),
            field_spec,
            pl.BlockSpec((4 * pairs, lon_count), lambda t: (0, 0)),
        ],
        out_specs=[field_spec, slot_spec(owners, slots)],
        out_shape=[
            jax.ShapeDtypeStruct(cotangent.shape, BF16),
            jax.ShapeDtypeStruct((owners, slots, lat_rows, 128), BF16),
        ],
        scratch_shapes=turn_scratch(pairs)
        + [
            pltpu.VMEM((4 * pairs, T_STEP * GROUP), BF16),
            pltpu.VMEM((T_STEP * GROUP, lon_count), BF16),
        ],
        compiler_params=params(46),
        cost_estimate=cost(25),
        name="middle_transform",
    )(pair_list, returned, cotangent, table)


def owned_tiles(degrees, chans, owners):
    return [divmod(tile, degrees // chans // owners) for tile in range(degrees // chans)]


def analysis_body(spread, owner_ref, pair_ref, in_ref, basis_ref, out_ref, lats_ref, rows_ref, *refs):
    step = pl.program_id(0)
    owners, steps, lat_rows, _ = in_ref.shape
    degrees = basis_ref.shape[1] - 1
    degree = lax.broadcasted_iota(jnp.int32, (degrees, 128), 0)
    is_first = lax.broadcasted_iota(jnp.int32, (degrees, 128), 1) < 64

    if spread:
        sent_ref = refs[0]

        @pl.when(step == 0)
        def _():
            sent_ref[...] = jnp.zeros_like(sent_ref)

    for k in range(steps):
        for owner in range(owners):
            lats_ref[k, owner * lat_rows : (owner + 1) * lat_rows, :] = in_ref[owner, k].astype(F32)
        rows_ref[k, degrees + 1 :, :] = jnp.zeros((7, 128), F32)
    for k in range(steps):
        spectrum = lats_ref[k].astype(BF16)
        rows_ref[k, : degrees + 1, :] = jnp.dot(
            basis_ref[k], spectrum, preferred_element_type=F32
        )
    for k in range(steps):
        slot = step * steps + k
        first = pair_ref[owner_ref[0] * pl.num_programs(0) * steps + slot]
        leading = pltpu.roll(rows_ref[k], first, 0)[:degrees]
        trailing = rows_ref[k, 1 : degrees + 1, :]
        smallest = jnp.where(is_first, first, degrees - 1 - first)
        table = jnp.where(degree >= smallest, jnp.where(is_first, leading, trailing), 0.0)
        if spread:
            block_rows = out_ref.shape[1]
            for tile, (i, s) in enumerate(owned_tiles(degrees, 8, owners)):
                row = 8 * i * block_rows + 3 * slot + s
                sent_ref[pl.ds(row, 8, stride=block_rows), :] = table[8 * tile : 8 * tile + 8]
        else:
            part = degrees // owners
            for owner in range(owners):
                out_ref[owner, k] = table[part * owner : part * (owner + 1)].astype(BF16)

    if spread:

        @pl.when(step == pl.num_programs(0) - 1)
        def _():
            out_ref[...] = sent_ref[...].astype(BF16).reshape(out_ref.shape)


def analysis(arrived, basis, places, spread):
    owners, slots, lat_rows, _ = arrived.shape
    _, rows, lat_total = basis.shape
    degrees = rows - 1
    scratch = [
        pltpu.VMEM((S_STEP, lat_total, 128), F32),
        pltpu.VMEM((S_STEP, degrees + 8, 128), F32),
    ]
    if spread:
        block_rows = round_up(3 * slots, 8)
        shape = (owners * 8, block_rows, 128)
        out_spec = pl.BlockSpec(shape, lambda k: (0, 0, 0))
        scratch.append(pltpu.VMEM((owners * 8 * block_rows, 128), F32))
    else:
        part = degrees // owners
        shape = (owners, slots, part, 128)
        out_spec = pl.BlockSpec((owners, S_STEP, part, 128), lambda k: (0, k, 0, 0))
    return pl.pallas_call(
        functools.partial(analysis_body, spread),
        grid=(slots // S_STEP,),
        in_specs=[
            pl.BlockSpec(memory_space=pltpu.SMEM),
            pl.BlockSpec(memory_space=pltpu.SMEM),
            pl.BlockSpec((owners, S_STEP, lat_rows, 128), lambda k: (0, k, 0, 0)),
            pl.BlockSpec((S_STEP, rows, lat_total), lambda k: (k, 0, 0)),
        ],
        out_specs=out_spec,
        out_shape=jax.ShapeDtypeStruct(shape, BF16),
        scratch_shapes=scratch,
        compiler_params=params(24),
        cost_estimate=cost(6),
        name="analysis",
    )(*places, arrived, basis)


def synthesis_body(owner_ref, pair_ref, in_ref, basis_ref, out_ref, held_ref, rows_ref, lats_ref):
    step = pl.program_id(0)
    owners, steps, lat_rows, _ = out_ref.shape
    degrees = basis_ref.shape[1] - 1
    block_rows = in_ref.shape[1]
    size = degrees + 8
    row = lax.broadcasted_iota(jnp.int32, (size, 128), 0)
    is_first = lax.broadcasted_iota(jnp.int32, (size, 128), 1) < 64

    @pl.when(step == 0)
    def _():
        held_ref[...] = in_ref[...].astype(F32).reshape(held_ref.shape)
        rows_ref[...] = jnp.zeros_like(rows_ref)

    for k in range(steps):
        slot = step * steps + k
        for tile, (i, s) in enumerate(owned_tiles(degrees, 8, owners)):
            start = 8 * i * block_rows + 3 * slot + s
            rows_ref[k, 8 * tile : 8 * tile + 8, :] = held_ref[pl.ds(start, 8, stride=block_rows), :]
    for k in range(steps):
        first = pair_ref[(owner_ref[0] * pl.num_programs(0) + step) * steps + k]
        table = rows_ref[k]
        leading = pltpu.roll(table, lax.rem(size - first, size), 0)
        trailing = pltpu.roll(table, 1, 0)
        lines = jnp.where(
            row < degrees - first,
            jnp.where(is_first, leading, 0.0),
            jnp.where(is_first, 0.0, trailing),
        )
        lats_ref[k] = tn_dot(basis_ref[k], lines[: degrees + 1].astype(BF16))
    for k in range(steps):
        for owner in range(owners):
            out_ref[owner, k] = lats_ref[k, owner * lat_rows : (owner + 1) * lat_rows, :].astype(BF16)


def synthesize(filtered, basis, places, owners, lat_rows):
    slots, rows, lat_total = basis.shape
    degrees = rows - 1
    devices, block_rows, _ = filtered.shape
    return pl.pallas_call(
        synthesis_body,
        grid=(slots // S_STEP,),
        in_specs=[
            pl.BlockSpec(memory_space=pltpu.SMEM),
            pl.BlockSpec(memory_space=pltpu.SMEM),
            pl.BlockSpec((devices, block_rows, 128), lambda k: (0, 0, 0)),
            pl.BlockSpec((S_STEP, rows, lat_total), lambda k: (k, 0, 0)),
        ],
        out_specs=pl.BlockSpec((owners, S_STEP, lat_rows, 128), lambda k: (0, k, 0, 0)),
        out_shape=jax.ShapeDtypeStruct((owners, slots, lat_rows, 128), BF16),
        scratch_shapes=[
            pltpu.VMEM((devices * block_rows, 128), F32),
            pltpu.VMEM((S_STEP, degrees + 8, 128), F32),
            pltpu.VMEM((S_STEP, lat_total, 128), F32),
        ],
        compiler_params=params(24),
        cost_estimate=cost(7),
        name="synthesis",
    )(*places, filtered, basis)


HELD = 48
OWNER_UNROLL = 2


def filter_body(slots, me_ref, in_ref, weight_ref, out_ref, degree_ref, rows_ref, kept_ref, tight_ref):
    devices, block_rows, _ = in_ref.shape
    owners = devices // 8

    def gather(owner, _):
        start = pl.multiple_of(owner * HELD, 8)
        for half in range(2):
            lanes = slice(128 * half, 128 * half + 128)
            tiles = [in_ref[owner * 8 + 4 * half + a].astype(F32) for a in range(4)]
            for hj, tile in enumerate(swap_groups(tiles)):
                rows_ref[hj, half, pl.ds(start, block_rows), :] = tile
                rows_ref[hj, half, pl.ds(start + block_rows, HELD - block_rows), :] = jnp.zeros(
                    (HELD - block_rows, 128), F32
                )
        return 0

    lax.fori_loop(0, owners, gather, 0, unroll=OWNER_UNROLL)
    per_owner = HELD // 3
    for s in range(3):
        weights = weight_ref[:, s, 0].reshape(256, 256)
        for hj in range(4):
            table = [
                rows_ref[hj, half, pl.ds(s, owners * per_owner, stride=3), :] for half in range(2)
            ]
            for half in range(2):
                for i in range(owners):
                    row = (hj * owners + i) * slots
                    tight_ref[row : row + slots, 128 * half : 128 * half + 128] = table[half][
                        per_owner * i : per_owner * i + slots
                    ]
            whole = jnp.concatenate([half.astype(BF16) for half in table], axis=1)
            product = nt_dot(whole, weights)
            for half in range(2):
                kept_ref[hj, half, pl.ds(s, owners * per_owner, stride=3), :] = product[
                    :, 128 * half : 128 * half + 128
                ]
        degree_ref[s] = tight_ref[...].astype(BF16)

    def scatter(owner, _):
        start = pl.multiple_of(owner * HELD, 8)
        for half in range(2):
            tiles = [kept_ref[hj, half, pl.ds(start, block_rows), :] for hj in range(4)]
            for a, tile in enumerate(swap_groups(tiles)):
                out_ref[owner * 8 + 4 * half + a] = tile.astype(BF16)
        return 0

    lax.fori_loop(0, owners, scatter, 0, unroll=OWNER_UNROLL)


def spectral_filter(received, weights, me, slots):
    devices, block_rows, _ = received.shape
    owners = devices // 8
    whole = lambda shape: pl.BlockSpec(shape, lambda n, me_ref: (0,) * len(shape))
    degree_shape = (3, 4 * owners * slots, 256)
    return pl.pallas_call(
        functools.partial(filter_body, slots),
        grid_spec=pltpu.PrefetchScalarGridSpec(
            num_scalar_prefetch=1,
            grid=(1,),
            in_specs=[
                whole(received.shape),
                pl.BlockSpec((8, 3, 1, GROUP, 256), lambda n, me_ref: (0, 0, me_ref[0], 0, 0)),
            ],
            out_specs=[whole(received.shape), whole(degree_shape)],
            scratch_shapes=[
                pltpu.VMEM((4, 2, owners * HELD, 128), F32),
                pltpu.VMEM((4, 2, owners * HELD, 128), F32),
                pltpu.VMEM((4 * owners * slots, 256), F32),
            ],
        ),
        out_shape=[
            jax.ShapeDtypeStruct(received.shape, BF16),
            jax.ShapeDtypeStruct(degree_shape, BF16),
        ],
        compiler_params=params(22),
        cost_estimate=cost(6),
        name="spectral_filter",
    )(me, received, weights)


def grad_body(in_ref, degree_ref, out_ref, rows_ref):
    step = pl.program_id(0)
    owners, slots, part, _ = in_ref.shape

    @pl.when(step == 0)
    def _():
        rows_ref[...] = in_ref[...].astype(F32).reshape(rows_ref.shape)

    group = lax.broadcasted_iota(jnp.int32, (owners * slots, 128), 1) // GROUP
    for j in range(8):
        grad = rows_ref[pl.ds(8 * step + j, owners * slots, stride=part), :]
        spread = [jnp.where(group == hj, grad, 0.0).astype(BF16) for hj in range(4)]
        sums = tn_dot(jnp.concatenate(spread, axis=0), degree_ref[j, 0])
        total = sums[:GROUP] + sums[GROUP : 2 * GROUP]
        out_ref[j] = total + (sums[2 * GROUP : 3 * GROUP] + sums[3 * GROUP :])


def filter_grad(received, by_degree):
    owners, slots, part, _ = received.shape
    chans, steps, rows, _ = by_degree.shape
    return pl.pallas_call(
        grad_body,
        grid=(steps,),
        in_specs=[
            pl.BlockSpec(received.shape, lambda s: (0, 0, 0, 0)),
            pl.BlockSpec((chans, 1, rows, 256), lambda s: (0, s, 0, 0)),
        ],
        out_specs=pl.BlockSpec((chans, GROUP, 256), lambda s: (s, 0, 0)),
        out_shape=jax.ShapeDtypeStruct((part, GROUP, 256), F32),
        scratch_shapes=[pltpu.VMEM((owners * slots * part, 128), F32)],
        compiler_params=params(40),
        cost_estimate=cost(6),
        name="filter_grad",
    )(received, by_degree)


def stay(array):
    return pltpu.with_memory_space_constraint(array, pltpu.HBM)


def exchange(array, axis):
    return lax.all_to_all(array, axis, split_axis=0, concat_axis=0, tiled=True)


def on_device(grid_in, lat_weights, legendre_basis, pair_list, filter_weights, cotangent):
    owners = lax.axis_size("lat")
    chans = lax.axis_size("chan")
    slots, rows, _ = legendre_basis.shape
    degrees = rows - 1
    _, lat_rows, chan_rows, lon_count = grid_in.shape
    grid, cotangent = grid_in[0], cotangent[0]
    owner = lax.axis_index("lat").reshape(1).astype(jnp.int32)
    me = lax.axis_index("chan").reshape(1).astype(jnp.int32)
    places = (owner, pair_list)
    table = longitude_table(degrees, lon_count, False)
    inverse_table = longitude_table(degrees, lon_count, True)

    everyone = ("lat", "chan")
    spectrum, weights = forward_transform(
        grid, lat_weights, pair_list, table, filter_weights, owner, owners, slots
    )
    weights = lax.all_gather(weights, "chan")
    weights = weights.reshape(chans, degrees // owners // chans, chans, chan_rows, -1)
    coefficients = analysis(exchange(spectrum, "lat"), stay(legendre_basis), places, True)
    filtered, by_degree = spectral_filter(exchange(coefficients, everyone), weights, me, slots)
    filtered, by_degree = lax.optimization_barrier((exchange(filtered, everyone), by_degree))
    by_degree = lax.all_gather(by_degree, "chan")
    lines = synthesize(filtered, stay(legendre_basis), places, owners, lat_rows)
    gate, grads = middle_transform(
        exchange(lines, "lat"), cotangent, pair_list, inverse_table, owners, slots
    )
    grads = analysis(exchange(grads, "lat"), legendre_basis, places, False)
    weight_grad = filter_grad(exchange(grads, "lat"), stay(by_degree))
    block_out = (grid.astype(F32) + gate.astype(F32)).astype(BF16)
    return (block_out[None], weight_grad)


def solution(mesh):
    in_specs = (
        P(None, "lat", "chan", None),
        P("lat"),
        P("lat", None, None),
        P(),
        P(None, "chan", None),
        P(None, "lat", "chan", None),
    )
    out_specs = (P(None, "lat", "chan", None), P("lat", "chan", None))
    return jax.shard_map(
        on_device, mesh=mesh, in_specs=in_specs, out_specs=out_specs, check_vma=False
    )
```

```python
import functools
import math

import jax
import jax.numpy as jnp
import numpy as np
from jax import lax
from jax.experimental import pallas as pl
from jax.experimental.pallas import tpu as pltpu
from jax.sharding import PartitionSpec as P

F32 = jnp.float32
BF16 = jnp.bfloat16
GROUP = 32
T_STEP = 16
T_PART = 8
S_STEP = 6


def params(mib):
    return pltpu.CompilerParams(vmem_limit_bytes=mib << 20)


def cost(microseconds):
    return pl.CostEstimate(
        flops=int(microseconds * 1e9), bytes_accessed=1 << 20, transcendentals=0
    )


def round_up(value, unit):
    return -(-value // unit) * unit


def longitude_table(degrees, lon_count, doubled):
    first = np.arange(degrees // 2)
    orders = np.stack([first, degrees - 1 - first])
    phases = orders[:, :, None] * np.arange(lon_count) % lon_count
    angles = phases * (2.0 * math.pi / lon_count)
    table = np.stack([np.cos(angles), -np.sin(angles)], axis=1) / math.sqrt(lon_count)
    if doubled:
        table = table * np.where(orders == 0, 1.0, 2.0)[:, None, :, None]
    return jnp.asarray(table.reshape(2 * degrees, lon_count).astype(np.float32)).astype(BF16)


def swap_groups(tiles):
    lane = lax.broadcasted_iota(jnp.int32, tiles[0].shape, 1)
    low, even = lane < 64, lane // GROUP % 2 == 0
    t0, t1, t2, t3 = tiles
    a0 = jnp.where(low, t0, pltpu.roll(t2, 64, 1))
    a1 = jnp.where(low, t1, pltpu.roll(t3, 64, 1))
    a2 = jnp.where(low, pltpu.roll(t0, 64, 1), t2)
    a3 = jnp.where(low, pltpu.roll(t1, 64, 1), t3)
    return [
        jnp.where(even, a0, pltpu.roll(a1, 32, 1)),
        jnp.where(even, pltpu.roll(a0, 96, 1), a1),
        jnp.where(even, a2, pltpu.roll(a3, 32, 1)),
        jnp.where(even, pltpu.roll(a2, 96, 1), a3),
    ]


P_BLOCK = 32
PAD = 1


def by_latitude(rows_ref, stacked_ref, pairs, part, weight_of):
    for start in range(0, pairs, P_BLOCK):
        for q in range(T_PART // 4):
            lanes = slice(128 * q, 128 * q + 128)
            tiles = [
                rows_ref[part, wi * pairs + start : wi * pairs + start + P_BLOCK, lanes]
                for wi in range(4)
            ]
            for s, tile in enumerate(swap_groups(tiles)):
                t = part * T_PART + 4 * q + s
                row = t * (pairs + PAD) + start
                stacked_ref[row : row + P_BLOCK, :] = tile if weight_of is None else tile * weight_of[t]


def by_order(stacked_ref, rows_ref, pairs, q):
    for start in range(0, pairs, P_BLOCK):
        tiles = []
        for s in range(4):
            row = (4 * q + s) * (pairs + PAD) + start
            tiles.append(stacked_ref[row : row + P_BLOCK, :])
        for wi, tile in enumerate(swap_groups(tiles)):
            row = wi * pairs + start
            rows_ref[row : row + P_BLOCK, 128 * q : 128 * q + 128] = tile.astype(BF16)


def send_slots(pair_ref, stacked_ref, out_ref, pairs, slots):
    def step(owner, _):
        for k in range(slots):
            order = pair_ref[owner * slots + k]
            tile = stacked_ref[pl.ds(order, T_STEP, stride=pairs + PAD), :]
            out_ref[owner, k] = tile.astype(BF16)
        return 0

    lax.fori_loop(0, pairs // slots, step, 0)


def nt_dot(a, b):
    return lax.dot_general(a, b, (((1,), (1,)), ((), ())), preferred_element_type=F32)


def tn_dot(a, b):
    return lax.dot_general(a, b, (((0,), (0,)), ((), ())), preferred_element_type=F32)


def forward_body(pairs, slots, lat_rows, owner_ref, pair_ref, weight_ref, *refs):
    grid_ref, table_ref, filter_ref, out_ref, part_ref, rows_ref, stacked_ref = refs
    start = pl.program_id(0) * T_STEP

    @pl.when(start == 0)
    def _():
        part_ref[...] = filter_ref[...]

    weight_of = [weight_ref[jnp.minimum(start + t, lat_rows - 1)] for t in range(T_STEP)]
    for part in range(T_STEP // T_PART):
        fields = grid_ref[part * T_PART : (part + 1) * T_PART].reshape(T_PART * GROUP, -1)
        rows_ref[part] = nt_dot(table_ref[...], fields)
        by_latitude(rows_ref, stacked_ref, pairs, part, weight_of)
    send_slots(pair_ref, stacked_ref, out_ref, pairs, slots)


def slot_spec(owners, slots):
    return pl.BlockSpec((owners, slots, T_STEP, 128), lambda t: (0, 0, t, 0))


def turn_scratch(pairs):
    return [
        pltpu.VMEM((T_STEP // T_PART, 4 * pairs, T_PART * GROUP), F32),
        pltpu.VMEM((round_up((T_STEP + 1) * (pairs + PAD), 8), 128), F32),
    ]


def forward_transform(grid, weights, pair_list, table, filters, owner, owners, slots):
    lat_rows, _, lon_count = grid.shape
    pairs = owners * slots
    part_shape = (filters.shape[0] // owners,) + filters.shape[1:]
    return pl.pallas_call(
        functools.partial(forward_body, pairs, slots, lat_rows),
        grid_spec=pltpu.PrefetchScalarGridSpec(
            num_scalar_prefetch=1,
            grid=(pl.cdiv(lat_rows, T_STEP),),
            in_specs=[
                pl.BlockSpec(memory_space=pltpu.SMEM),
                pl.BlockSpec(memory_space=pltpu.SMEM),
                pl.BlockSpec((T_STEP, GROUP, lon_count), lambda t, owner_ref: (t, 0, 0)),
                pl.BlockSpec((4 * pairs, lon_count), lambda t, owner_ref: (0, 0)),
                pl.BlockSpec(part_shape, lambda t, owner_ref: (owner_ref[0], 0, 0)),
            ],
            out_specs=[
                pl.BlockSpec((owners, slots, T_STEP, 128), lambda t, owner_ref: (0, 0, t, 0)),
                pl.BlockSpec(part_shape, lambda t, owner_ref: (0, 0, 0)),
            ],
            scratch_shapes=turn_scratch(pairs),
        ),
        out_shape=[
            jax.ShapeDtypeStruct((owners, slots, lat_rows, 128), BF16),
            jax.ShapeDtypeStruct(part_shape, BF16),
        ],
        compiler_params=params(56),
        cost_estimate=cost(12),
        name="forward_transform",
    )(owner, pair_list, weights, grid, table, filters)


def middle_body(pairs, slots, pair_ref, in_ref, cot_ref, table_ref, *refs):
    field_ref, out_ref, rows_ref, stacked_ref, lines_ref, grad_ref = refs

    def step(owner, _):
        for k in range(slots):
            order = pair_ref[owner * slots + k]
            tile = in_ref[owner, k].astype(F32)
            stacked_ref[pl.ds(order, T_STEP, stride=pairs + PAD), :] = tile
        return 0

    lax.fori_loop(0, pairs // slots, step, 0)
    root = math.sqrt(2.0 / math.pi)
    for q in range(T_STEP // 4):
        by_order(stacked_ref, lines_ref, pairs, q)
        rows = slice(128 * q, 128 * q + 128)
        lats = slice(4 * q, 4 * q + 4)
        x = tn_dot(lines_ref[:, rows], table_ref[...])
        square = x * x
        th = jnp.tanh(x * (root + (root * 0.044715) * square))
        half = 0.5 + 0.5 * th
        gate = x * half
        slope = half + gate * (1.0 - th) * (root + (3.0 * root * 0.044715) * square)
        field_ref[lats] = gate.astype(BF16).reshape(4, GROUP, -1)
        cot = cot_ref[lats].reshape(128, -1).astype(F32)
        grad_ref[rows, :] = (cot * slope).astype(BF16)
    for part in range(T_STEP // T_PART):
        grads = grad_ref[part * T_PART * GROUP : (part + 1) * T_PART * GROUP, :]
        rows_ref[part] = nt_dot(table_ref[...], grads)
        by_latitude(rows_ref, stacked_ref, pairs, part, None)
    send_slots(pair_ref, stacked_ref, out_ref, pairs, slots)


def middle_transform(returned, cotangent, pair_list, table, owners, slots):
    lat_rows, _, lon_count = cotangent.shape
    pairs = owners * slots
    field_spec = pl.BlockSpec((T_STEP, GROUP, lon_count), lambda t: (t, 0, 0))
    return pl.pallas_call(
        functools.partial(middle_body, pairs, slots),
        grid=(pl.cdiv(lat_rows, T_STEP),),
        in_specs=[
            pl.BlockSpec(memory_space=pltpu.SMEM),
            slot_spec(owners, slots),
            field_spec,
            pl.BlockSpec((4 * pairs, lon_count), lambda t: (0, 0)),
        ],
        out_specs=[field_spec, slot_spec(owners, slots)],
        out_shape=[
            jax.ShapeDtypeStruct(cotangent.shape, BF16),
            jax.ShapeDtypeStruct((owners, slots, lat_rows, 128), BF16),
        ],
        scratch_shapes=turn_scratch(pairs)
        + [
            pltpu.VMEM((4 * pairs, T_STEP * GROUP), BF16),
            pltpu.VMEM((T_STEP * GROUP, lon_count), BF16),
        ],
        compiler_params=params(46),
        cost_estimate=cost(25),
        name="middle_transform",
    )(pair_list, returned, cotangent, table)


def owned_tiles(degrees, chans, owners):
    return [divmod(tile, degrees // chans // owners) for tile in range(degrees // chans)]


def analysis_body(spread, owner_ref, pair_ref, in_ref, basis_ref, out_ref, lats_ref, rows_ref, *refs):
    step = pl.program_id(0)
    owners, steps, lat_rows, _ = in_ref.shape
    degrees = basis_ref.shape[1] - 1
    degree = lax.broadcasted_iota(jnp.int32, (degrees, 128), 0)
    is_first = lax.broadcasted_iota(jnp.int32, (degrees, 128), 1) < 64

    if spread:
        sent_ref = refs[0]

        @pl.when(step == 0)
        def _():
            sent_ref[...] = jnp.zeros_like(sent_ref)

    for k in range(steps):
        for owner in range(owners):
            lats_ref[k, owner * lat_rows : (owner + 1) * lat_rows, :] = in_ref[owner, k].astype(F32)
        rows_ref[k, degrees + 1 :, :] = jnp.zeros((7, 128), F32)
    for k in range(steps):
        spectrum = lats_ref[k].astype(BF16)
        rows_ref[k, : degrees + 1, :] = jnp.dot(
            basis_ref[k], spectrum, preferred_element_type=F32
        )
    for k in range(steps):
        slot = step * steps + k
        first = pair_ref[owner_ref[0] * pl.num_programs(0) * steps + slot]
        leading = pltpu.roll(rows_ref[k], first, 0)[:degrees]
        trailing = rows_ref[k, 1 : degrees + 1, :]
        smallest = jnp.where(is_first, first, degrees - 1 - first)
        table = jnp.where(degree >= smallest, jnp.where(is_first, leading, trailing), 0.0)
        if spread:
            block_rows = out_ref.shape[1]
            for tile, (i, s) in enumerate(owned_tiles(degrees, 8, owners)):
                row = 8 * i * block_rows + 3 * slot + s
                sent_ref[pl.ds(row, 8, stride=block_rows), :] = table[8 * tile : 8 * tile + 8]
        else:
            part = degrees // owners
            for owner in range(owners):
                out_ref[owner, k] = table[part * owner : part * (owner + 1)].astype(BF16)

    if spread:

        @pl.when(step == pl.num_programs(0) - 1)
        def _():
            sent = sent_ref[: out_ref.shape[0] * out_ref.shape[1], :]
            out_ref[...] = sent.astype(BF16).reshape(out_ref.shape)


def analysis(arrived, basis, places, spread):
    owners, slots, lat_rows, _ = arrived.shape
    _, rows, lat_total = basis.shape
    degrees = rows - 1
    scratch = [
        pltpu.VMEM((S_STEP, lat_total, 128), F32),
        pltpu.VMEM((S_STEP, degrees + 8, 128), F32),
    ]
    if spread:
        block_rows = round_up(3 * slots, 8)
        shape = (owners * 8, block_rows, 128)
        out_spec = pl.BlockSpec(shape, lambda k: (0, 0, 0))
        scratch.append(pltpu.VMEM(((owners * 8 + 1) * block_rows, 128), F32))
    else:
        part = degrees // owners
        shape = (owners, slots, part, 128)
        out_spec = pl.BlockSpec((owners, S_STEP, part, 128), lambda k: (0, k, 0, 0))
    return pl.pallas_call(
        functools.partial(analysis_body, spread),
        grid=(slots // S_STEP,),
        in_specs=[
            pl.BlockSpec(memory_space=pltpu.SMEM),
            pl.BlockSpec(memory_space=pltpu.SMEM),
            pl.BlockSpec((owners, S_STEP, lat_rows, 128), lambda k: (0, k, 0, 0)),
            pl.BlockSpec((S_STEP, rows, lat_total), lambda k: (k, 0, 0)),
        ],
        out_specs=out_spec,
        out_shape=jax.ShapeDtypeStruct(shape, BF16),
        scratch_shapes=scratch,
        compiler_params=params(24),
        cost_estimate=cost(6),
        name="analysis",
    )(*places, arrived, basis)


def synthesis_body(owner_ref, pair_ref, in_ref, basis_ref, out_ref, held_ref, rows_ref, lats_ref):
    step = pl.program_id(0)
    owners, steps, lat_rows, _ = out_ref.shape
    degrees = basis_ref.shape[1] - 1
    block_rows = in_ref.shape[1]
    size = degrees + 8
    row = lax.broadcasted_iota(jnp.int32, (size, 128), 0)
    is_first = lax.broadcasted_iota(jnp.int32, (size, 128), 1) < 64

    @pl.when(step == 0)
    def _():
        held_ref[: in_ref.shape[0] * block_rows, :] = in_ref[...].astype(F32).reshape(-1, 128)
        rows_ref[...] = jnp.zeros_like(rows_ref)

    for k in range(steps):
        slot = step * steps + k
        for tile, (i, s) in enumerate(owned_tiles(degrees, 8, owners)):
            start = 8 * i * block_rows + 3 * slot + s
            rows_ref[k, 8 * tile : 8 * tile + 8, :] = held_ref[pl.ds(start, 8, stride=block_rows), :]
    for k in range(steps):
        first = pair_ref[(owner_ref[0] * pl.num_programs(0) + step) * steps + k]
        table = rows_ref[k]
        leading = pltpu.roll(table, lax.rem(size - first, size), 0)
        trailing = pltpu.roll(table, 1, 0)
        lines = jnp.where(
            row < degrees - first,
            jnp.where(is_first, leading, 0.0),
            jnp.where(is_first, 0.0, trailing),
        )
        lats_ref[k] = tn_dot(basis_ref[k], lines[: degrees + 1].astype(BF16))
    for k in range(steps):
        for owner in range(owners):
            out_ref[owner, k] = lats_ref[k, owner * lat_rows : (owner + 1) * lat_rows, :].astype(BF16)


def synthesize(filtered, basis, places, owners, lat_rows):
    slots, rows, lat_total = basis.shape
    degrees = rows - 1
    devices, block_rows, _ = filtered.shape
    return pl.pallas_call(
        synthesis_body,
        grid=(slots // S_STEP,),
        in_specs=[
            pl.BlockSpec(memory_space=pltpu.SMEM),
            pl.BlockSpec(memory_space=pltpu.SMEM),
            pl.BlockSpec((devices, block_rows, 128), lambda k: (0, 0, 0)),
            pl.BlockSpec((S_STEP, rows, lat_total), lambda k: (k, 0, 0)),
        ],
        out_specs=pl.BlockSpec((owners, S_STEP, lat_rows, 128), lambda k: (0, k, 0, 0)),
        out_shape=jax.ShapeDtypeStruct((owners, slots, lat_rows, 128), BF16),
        scratch_shapes=[
            pltpu.VMEM(((devices + 1) * block_rows, 128), F32),
            pltpu.VMEM((S_STEP, degrees + 8, 128), F32),
            pltpu.VMEM((S_STEP, lat_total, 128), F32),
        ],
        compiler_params=params(24),
        cost_estimate=cost(7),
        name="synthesis",
    )(*places, filtered, basis)


HELD = 48
OWNER_UNROLL = 2


def filter_body(slots, me_ref, in_ref, weight_ref, out_ref, degree_ref, rows_ref, kept_ref, tight_ref):
    devices, block_rows, _ = in_ref.shape
    owners = devices // 8

    def gather(owner, _):
        start = pl.multiple_of(owner * HELD, 8)
        for half in range(2):
            lanes = slice(128 * half, 128 * half + 128)
            tiles = [in_ref[owner * 8 + 4 * half + a].astype(F32) for a in range(4)]
            for hj, tile in enumerate(swap_groups(tiles)):
                rows_ref[hj, half, pl.ds(start, block_rows), :] = tile
                rows_ref[hj, half, pl.ds(start + block_rows, HELD - block_rows), :] = jnp.zeros(
                    (HELD - block_rows, 128), F32
                )
        return 0

    lax.fori_loop(0, owners, gather, 0, unroll=OWNER_UNROLL)
    per_owner = HELD // 3
    for s in range(3):
        weights = weight_ref[:, s, 0].reshape(256, 256)
        for hj in range(4):
            table = [
                rows_ref[hj, half, pl.ds(s, owners * per_owner, stride=3), :] for half in range(2)
            ]
            for half in range(2):
                for i in range(owners):
                    row = (hj * owners + i) * slots
                    tight_ref[row : row + slots, 128 * half : 128 * half + 128] = table[half][
                        per_owner * i : per_owner * i + slots
                    ]
            whole = jnp.concatenate([half.astype(BF16) for half in table], axis=1)
            product = nt_dot(whole, weights)
            for half in range(2):
                kept_ref[hj, half, pl.ds(s, owners * per_owner, stride=3), :] = product[
                    :, 128 * half : 128 * half + 128
                ]
        degree_ref[s] = tight_ref[...].astype(BF16)

    def scatter(owner, _):
        start = pl.multiple_of(owner * HELD, 8)
        for half in range(2):
            tiles = [kept_ref[hj, half, pl.ds(start, block_rows), :] for hj in range(4)]
            for a, tile in enumerate(swap_groups(tiles)):
                out_ref[owner * 8 + 4 * half + a] = tile.astype(BF16)
        return 0

    lax.fori_loop(0, owners, scatter, 0, unroll=OWNER_UNROLL)


def spectral_filter(received, weights, me, slots):
    devices, block_rows, _ = received.shape
    owners = devices // 8
    whole = lambda shape: pl.BlockSpec(shape, lambda n, me_ref: (0,) * len(shape))
    degree_shape = (3, 4 * owners * slots, 256)
    return pl.pallas_call(
        functools.partial(filter_body, slots),
        grid_spec=pltpu.PrefetchScalarGridSpec(
            num_scalar_prefetch=1,
            grid=(1,),
            in_specs=[
                whole(received.shape),
                pl.BlockSpec((8, 3, 1, GROUP, 256), lambda n, me_ref: (0, 0, me_ref[0], 0, 0)),
            ],
            out_specs=[whole(received.shape), whole(degree_shape)],
            scratch_shapes=[
                pltpu.VMEM((4, 2, owners * HELD + 8, 128), F32),
                pltpu.VMEM((4, 2, owners * HELD + 8, 128), F32),
                pltpu.VMEM((4 * owners * slots, 256), F32),
            ],
        ),
        out_shape=[
            jax.ShapeDtypeStruct(received.shape, BF16),
            jax.ShapeDtypeStruct(degree_shape, BF16),
        ],
        compiler_params=params(22),
        cost_estimate=cost(6),
        name="spectral_filter",
    )(me, received, weights)


def grad_body(in_ref, degree_ref, out_ref, rows_ref):
    step = pl.program_id(0)
    owners, slots, part, _ = in_ref.shape

    @pl.when(step == 0)
    def _():
        rows_ref[: owners * slots * part, :] = in_ref[...].astype(F32).reshape(-1, 128)

    group = lax.broadcasted_iota(jnp.int32, (owners * slots, 128), 1) // GROUP
    for j in range(8):
        grad = rows_ref[pl.ds(8 * step + j, owners * slots, stride=part), :]
        spread = [jnp.where(group == hj, grad, 0.0).astype(BF16) for hj in range(4)]
        sums = tn_dot(jnp.concatenate(spread, axis=0), degree_ref[j, 0])
        total = sums[:GROUP] + sums[GROUP : 2 * GROUP]
        out_ref[j] = total + (sums[2 * GROUP : 3 * GROUP] + sums[3 * GROUP :])


def filter_grad(received, by_degree):
    owners, slots, part, _ = received.shape
    chans, steps, rows, _ = by_degree.shape
    return pl.pallas_call(
        grad_body,
        grid=(steps,),
        in_specs=[
            pl.BlockSpec(received.shape, lambda s: (0, 0, 0, 0)),
            pl.BlockSpec((chans, 1, rows, 256), lambda s: (0, s, 0, 0)),
        ],
        out_specs=pl.BlockSpec((chans, GROUP, 256), lambda s: (s, 0, 0)),
        out_shape=jax.ShapeDtypeStruct((part, GROUP, 256), F32),
        scratch_shapes=[pltpu.VMEM(((owners * slots + 1) * part, 128), F32)],
        compiler_params=params(40),
        cost_estimate=cost(6),
        name="filter_grad",
    )(received, by_degree)


def stay(array):
    return pltpu.with_memory_space_constraint(array, pltpu.HBM)


def exchange(array, axis):
    return lax.all_to_all(array, axis, split_axis=0, concat_axis=0, tiled=True)


def on_device(grid_in, lat_weights, legendre_basis, pair_list, filter_weights, cotangent):
    owners = lax.axis_size("lat")
    chans = lax.axis_size("chan")
    slots, rows, _ = legendre_basis.shape
    degrees = rows - 1
    _, lat_rows, chan_rows, lon_count = grid_in.shape
    grid, cotangent = grid_in[0], cotangent[0]
    owner = lax.axis_index("lat").reshape(1).astype(jnp.int32)
    me = lax.axis_index("chan").reshape(1).astype(jnp.int32)
    places = (owner, pair_list)
    table = longitude_table(degrees, lon_count, False)
    inverse_table = longitude_table(degrees, lon_count, True)

    everyone = ("lat", "chan")
    spectrum, weights = forward_transform(
        grid, lat_weights, pair_list, table, filter_weights, owner, owners, slots
    )
    weights = lax.all_gather(weights, "chan")
    weights = weights.reshape(chans, degrees // owners // chans, chans, chan_rows, -1)
    coefficients = analysis(exchange(spectrum, "lat"), stay(legendre_basis), places, True)
    filtered, by_degree = spectral_filter(exchange(coefficients, everyone), weights, me, slots)
    filtered, by_degree = lax.optimization_barrier((exchange(filtered, everyone), by_degree))
    by_degree = lax.all_gather(by_degree, "chan")
    lines = synthesize(filtered, stay(legendre_basis), places, owners, lat_rows)
    gate, grads = middle_transform(
        exchange(lines, "lat"), cotangent, pair_list, inverse_table, owners, slots
    )
    grads = analysis(exchange(grads, "lat"), legendre_basis, places, False)
    weight_grad = filter_grad(exchange(grads, "lat"), stay(by_degree))
    block_out = (grid.astype(F32) + gate.astype(F32)).astype(BF16)
    return (block_out[None], weight_grad)


def solution(mesh):
    in_specs = (
        P(None, "lat", "chan", None),
        P("lat"),
        P("lat", None, None),
        P(),
        P(None, "chan", None),
        P(None, "lat", "chan", None),
    )
    out_specs = (P(None, "lat", "chan", None), P("lat", "chan", None))
    return jax.shard_map(
        on_device, mesh=mesh, in_specs=in_specs, out_specs=out_specs, check_vma=False
    )
```

```python
import functools
import math

import jax
import jax.numpy as jnp
import numpy as np
from jax import lax
from jax.experimental import pallas as pl
from jax.experimental.pallas import tpu as pltpu
from jax.sharding import PartitionSpec as P

F32 = jnp.float32
BF16 = jnp.bfloat16
GROUP = 32
T_STEP = 16
T_PART = 16
S_STEP = 6


def params(mib):
    return pltpu.CompilerParams(vmem_limit_bytes=mib << 20)


def cost(microseconds):
    return pl.CostEstimate(
        flops=int(microseconds * 1e9), bytes_accessed=1 << 20, transcendentals=0
    )


def round_up(value, unit):
    return -(-value // unit) * unit


def longitude_table(degrees, lon_count, doubled):
    first = np.arange(degrees // 2)
    orders = np.stack([first, degrees - 1 - first])
    phases = orders[:, :, None] * np.arange(lon_count) % lon_count
    angles = phases * (2.0 * math.pi / lon_count)
    table = np.stack([np.cos(angles), -np.sin(angles)], axis=1) / math.sqrt(lon_count)
    if doubled:
        table = table * np.where(orders == 0, 1.0, 2.0)[:, None, :, None]
    return jnp.asarray(table.reshape(2 * degrees, lon_count).astype(np.float32)).astype(BF16)


def swap_groups(tiles):
    lane = lax.broadcasted_iota(jnp.int32, tiles[0].shape, 1)
    low, even = lane < 64, lane // GROUP % 2 == 0
    t0, t1, t2, t3 = tiles
    a0 = jnp.where(low, t0, pltpu.roll(t2, 64, 1))
    a1 = jnp.where(low, t1, pltpu.roll(t3, 64, 1))
    a2 = jnp.where(low, pltpu.roll(t0, 64, 1), t2)
    a3 = jnp.where(low, pltpu.roll(t1, 64, 1), t3)
    return [
        jnp.where(even, a0, pltpu.roll(a1, 32, 1)),
        jnp.where(even, pltpu.roll(a0, 96, 1), a1),
        jnp.where(even, a2, pltpu.roll(a3, 32, 1)),
        jnp.where(even, pltpu.roll(a2, 96, 1), a3),
    ]


P_BLOCK = 32
PAD = 1


def by_latitude(rows_ref, stacked_ref, pairs, part, weight_of):
    for start in range(0, pairs, P_BLOCK):
        for q in range(T_PART // 4):
            lanes = slice(128 * q, 128 * q + 128)
            tiles = [
                rows_ref[part, wi * pairs + start : wi * pairs + start + P_BLOCK, lanes]
                for wi in range(4)
            ]
            for s, tile in enumerate(swap_groups(tiles)):
                t = part * T_PART + 4 * q + s
                row = t * (pairs + PAD) + start
                stacked_ref[row : row + P_BLOCK, :] = tile if weight_of is None else tile * weight_of[t]


def by_order(stacked_ref, rows_ref, pairs, q):
    for start in range(0, pairs, P_BLOCK):
        tiles = []
        for s in range(4):
            row = (4 * q + s) * (pairs + PAD) + start
            tiles.append(stacked_ref[row : row + P_BLOCK, :])
        for wi, tile in enumerate(swap_groups(tiles)):
            row = wi * pairs + start
            rows_ref[row : row + P_BLOCK, 128 * q : 128 * q + 128] = tile.astype(BF16)


def send_slots(pair_ref, stacked_ref, out_ref, pairs, slots):
    def step(owner, _):
        for k in range(slots):
            order = pair_ref[owner * slots + k]
            tile = stacked_ref[pl.ds(order, T_STEP, stride=pairs + PAD), :]
            out_ref[owner, k] = tile.astype(BF16)
        return 0

    lax.fori_loop(0, pairs // slots, step, 0)


def nt_dot(a, b):
    return lax.dot_general(a, b, (((1,), (1,)), ((), ())), preferred_element_type=F32)


def tn_dot(a, b):
    return lax.dot_general(a, b, (((0,), (0,)), ((), ())), preferred_element_type=F32)


def forward_body(pairs, slots, lat_rows, owner_ref, pair_ref, weight_ref, *refs):
    grid_ref, table_ref, filter_ref, out_ref, part_ref, rows_ref, stacked_ref = refs
    start = pl.program_id(0) * T_STEP

    @pl.when(start == 0)
    def _():
        part_ref[...] = filter_ref[...]

    weight_of = [weight_ref[jnp.minimum(start + t, lat_rows - 1)] for t in range(T_STEP)]
    for part in range(T_STEP // T_PART):
        fields = grid_ref[part * T_PART : (part + 1) * T_PART].reshape(T_PART * GROUP, -1)
        rows_ref[part] = nt_dot(table_ref[...], fields)
        by_latitude(rows_ref, stacked_ref, pairs, part, weight_of)
    send_slots(pair_ref, stacked_ref, out_ref, pairs, slots)


def slot_spec(owners, slots):
    return pl.BlockSpec((owners, slots, T_STEP, 128), lambda t: (0, 0, t, 0))


def turn_scratch(pairs):
    return [
        pltpu.VMEM((T_STEP // T_PART, 4 * pairs, T_PART * GROUP), F32),
        pltpu.VMEM((round_up((T_STEP + 1) * (pairs + PAD), 8), 128), F32),
    ]


def forward_transform(grid, weights, pair_list, table, filters, owner, owners, slots):
    lat_rows, _, lon_count = grid.shape
    pairs = owners * slots
    part_shape = (filters.shape[0] // owners,) + filters.shape[1:]
    return pl.pallas_call(
        functools.partial(forward_body, pairs, slots, lat_rows),
        grid_spec=pltpu.PrefetchScalarGridSpec(
            num_scalar_prefetch=1,
            grid=(pl.cdiv(lat_rows, T_STEP),),
            in_specs=[
                pl.BlockSpec(memory_space=pltpu.SMEM),
                pl.BlockSpec(memory_space=pltpu.SMEM),
                pl.BlockSpec((T_STEP, GROUP, lon_count), lambda t, owner_ref: (t, 0, 0)),
                pl.BlockSpec((4 * pairs, lon_count), lambda t, owner_ref: (0, 0)),
                pl.BlockSpec(part_shape, lambda t, owner_ref: (owner_ref[0], 0, 0)),
            ],
            out_specs=[
                pl.BlockSpec((owners, slots, T_STEP, 128), lambda t, owner_ref: (0, 0, t, 0)),
                pl.BlockSpec(part_shape, lambda t, owner_ref: (0, 0, 0)),
            ],
            scratch_shapes=turn_scratch(pairs),
        ),
        out_shape=[
            jax.ShapeDtypeStruct((owners, slots, lat_rows, 128), BF16),
            jax.ShapeDtypeStruct(part_shape, BF16),
        ],
        compiler_params=params(56),
        cost_estimate=cost(12),
        name="forward_transform",
    )(owner, pair_list, weights, grid, table, filters)


def middle_body(pairs, slots, pair_ref, in_ref, cot_ref, table_ref, *refs):
    field_ref, out_ref, rows_ref, stacked_ref, lines_ref, grad_ref = refs

    def step(owner, _):
        for k in range(slots):
            order = pair_ref[owner * slots + k]
            tile = in_ref[owner, k].astype(F32)
            stacked_ref[pl.ds(order, T_STEP, stride=pairs + PAD), :] = tile
        return 0

    lax.fori_loop(0, pairs // slots, step, 0)
    root = math.sqrt(2.0 / math.pi)
    for q in range(T_STEP // 4):
        by_order(stacked_ref, lines_ref, pairs, q)
        rows = slice(128 * q, 128 * q + 128)
        lats = slice(4 * q, 4 * q + 4)
        x = tn_dot(lines_ref[:, rows], table_ref[...])
        square = x * x
        th = jnp.tanh(x * (root + (root * 0.044715) * square))
        half = 0.5 + 0.5 * th
        gate = x * half
        slope = half + gate * (1.0 - th) * (root + (3.0 * root * 0.044715) * square)
        field_ref[lats] = gate.astype(BF16).reshape(4, GROUP, -1)
        cot = cot_ref[lats].reshape(128, -1).astype(F32)
        grad_ref[rows, :] = (cot * slope).astype(BF16)
    for part in range(T_STEP // T_PART):
        grads = grad_ref[part * T_PART * GROUP : (part + 1) * T_PART * GROUP, :]
        rows_ref[part] = nt_dot(table_ref[...], grads)
        by_latitude(rows_ref, stacked_ref, pairs, part, None)
    send_slots(pair_ref, stacked_ref, out_ref, pairs, slots)


def middle_transform(returned, cotangent, pair_list, table, owners, slots):
    lat_rows, _, lon_count = cotangent.shape
    pairs = owners * slots
    field_spec = pl.BlockSpec((T_STEP, GROUP, lon_count), lambda t: (t, 0, 0))
    return pl.pallas_call(
        functools.partial(middle_body, pairs, slots),
        grid=(pl.cdiv(lat_rows, T_STEP),),
        in_specs=[
            pl.BlockSpec(memory_space=pltpu.SMEM),
            slot_spec(owners, slots),
            field_spec,
            pl.BlockSpec((4 * pairs, lon_count), lambda t: (0, 0)),
        ],
        out_specs=[field_spec, slot_spec(owners, slots)],
        out_shape=[
            jax.ShapeDtypeStruct(cotangent.shape, BF16),
            jax.ShapeDtypeStruct((owners, slots, lat_rows, 128), BF16),
        ],
        scratch_shapes=turn_scratch(pairs)
        + [
            pltpu.VMEM((4 * pairs, T_STEP * GROUP), BF16),
            pltpu.VMEM((T_STEP * GROUP, lon_count), BF16),
        ],
        compiler_params=params(46),
        cost_estimate=cost(25),
        name="middle_transform",
    )(pair_list, returned, cotangent, table)


def owned_tiles(degrees, chans, owners):
    return [divmod(tile, degrees // chans // owners) for tile in range(degrees // chans)]


def analysis_body(spread, used_rows, owner_ref, pair_ref, in_ref, basis_ref, out_ref, lats_ref, rows_ref, *refs):
    step = pl.program_id(0)
    owners, steps, lat_rows, _ = in_ref.shape
    degrees = basis_ref.shape[1] - 1
    degree = lax.broadcasted_iota(jnp.int32, (degrees, 128), 0)
    is_first = lax.broadcasted_iota(jnp.int32, (degrees, 128), 1) < 64

    if spread:
        sent_ref = refs[0]

        @pl.when(step == 0)
        def _():
            devices, block_rows, _ = out_ref.shape
            for row in range(used_rows, block_rows):
                sent_ref[pl.ds(row, devices, stride=block_rows), :] = jnp.zeros((devices, 128), F32)

    for k in range(steps):
        for owner in range(owners):
            lats_ref[k, owner * lat_rows : (owner + 1) * lat_rows, :] = in_ref[owner, k].astype(F32)
        rows_ref[k, degrees + 1 :, :] = jnp.zeros((7, 128), F32)
    for k in range(steps):
        spectrum = lats_ref[k].astype(BF16)
        rows_ref[k, : degrees + 1, :] = jnp.dot(
            basis_ref[k], spectrum, preferred_element_type=F32
        )
    for k in range(steps):
        slot = step * steps + k
        first = pair_ref[owner_ref[0] * pl.num_programs(0) * steps + slot]
        leading = pltpu.roll(rows_ref[k], first, 0)[:degrees]
        trailing = rows_ref[k, 1 : degrees + 1, :]
        smallest = jnp.where(is_first, first, degrees - 1 - first)
        table = jnp.where(degree >= smallest, jnp.where(is_first, leading, trailing), 0.0)
        if spread:
            block_rows = out_ref.shape[1]
            for tile, (i, s) in enumerate(owned_tiles(degrees, 8, owners)):
                row = 8 * i * block_rows + 3 * slot + s
                sent_ref[pl.ds(row, 8, stride=block_rows), :] = table[8 * tile : 8 * tile + 8]
        else:
            part = degrees // owners
            for owner in range(owners):
                out_ref[owner, k] = table[part * owner : part * (owner + 1)].astype(BF16)

    if spread:

        @pl.when(step == pl.num_programs(0) - 1)
        def _():
            sent = sent_ref[: out_ref.shape[0] * out_ref.shape[1], :]
            out_ref[...] = sent.astype(BF16).reshape(out_ref.shape)


def analysis(arrived, basis, places, spread):
    owners, slots, lat_rows, _ = arrived.shape
    _, rows, lat_total = basis.shape
    degrees = rows - 1
    scratch = [
        pltpu.VMEM((S_STEP, lat_total, 128), F32),
        pltpu.VMEM((S_STEP, degrees + 8, 128), F32),
    ]
    if spread:
        block_rows = round_up(3 * slots, 8)
        shape = (owners * 8, block_rows, 128)
        out_spec = pl.BlockSpec(shape, lambda k: (0, 0, 0))
        scratch.append(pltpu.VMEM(((owners * 8 + 1) * block_rows, 128), F32))
    else:
        part = degrees // owners
        shape = (owners, slots, part, 128)
        out_spec = pl.BlockSpec((owners, S_STEP, part, 128), lambda k: (0, k, 0, 0))
    return pl.pallas_call(
        functools.partial(analysis_body, spread, 3 * slots),
        grid=(slots // S_STEP,),
        in_specs=[
            pl.BlockSpec(memory_space=pltpu.SMEM),
            pl.BlockSpec(memory_space=pltpu.SMEM),
            pl.BlockSpec((owners, S_STEP, lat_rows, 128), lambda k: (0, k, 0, 0)),
            pl.BlockSpec((S_STEP, rows, lat_total), lambda k: (k, 0, 0)),
        ],
        out_specs=out_spec,
        out_shape=jax.ShapeDtypeStruct(shape, BF16),
        scratch_shapes=scratch,
        compiler_params=params(24),
        cost_estimate=cost(6),
        name="analysis",
    )(*places, arrived, basis)


def synthesis_body(owner_ref, pair_ref, in_ref, basis_ref, out_ref, held_ref, rows_ref, lats_ref):
    step = pl.program_id(0)
    owners, steps, lat_rows, _ = out_ref.shape
    degrees = basis_ref.shape[1] - 1
    block_rows = in_ref.shape[1]
    size = degrees + 8
    row = lax.broadcasted_iota(jnp.int32, (size, 128), 0)
    is_first = lax.broadcasted_iota(jnp.int32, (size, 128), 1) < 64

    @pl.when(step == 0)
    def _():
        held_ref[: in_ref.shape[0] * block_rows, :] = in_ref[...].astype(F32).reshape(-1, 128)
        rows_ref[:, degrees:, :] = jnp.zeros((steps, size - degrees, 128), F32)

    for k in range(steps):
        slot = step * steps + k
        for tile, (i, s) in enumerate(owned_tiles(degrees, 8, owners)):
            start = 8 * i * block_rows + 3 * slot + s
            rows_ref[k, 8 * tile : 8 * tile + 8, :] = held_ref[pl.ds(start, 8, stride=block_rows), :]
    for k in range(steps):
        first = pair_ref[(owner_ref[0] * pl.num_programs(0) + step) * steps + k]
        table = rows_ref[k]
        leading = pltpu.roll(table, lax.rem(size - first, size), 0)
        trailing = pltpu.roll(table, 1, 0)
        lines = jnp.where(
            row < degrees - first,
            jnp.where(is_first, leading, 0.0),
            jnp.where(is_first, 0.0, trailing),
        )
        lats_ref[k] = tn_dot(basis_ref[k], lines[: degrees + 1].astype(BF16))
    for k in range(steps):
        for owner in range(owners):
            out_ref[owner, k] = lats_ref[k, owner * lat_rows : (owner + 1) * lat_rows, :].astype(BF16)


def synthesize(filtered, basis, places, owners, lat_rows):
    slots, rows, lat_total = basis.shape
    degrees = rows - 1
    devices, block_rows, _ = filtered.shape
    return pl.pallas_call(
        synthesis_body,
        grid=(slots // S_STEP,),
        in_specs=[
            pl.BlockSpec(memory_space=pltpu.SMEM),
            pl.BlockSpec(memory_space=pltpu.SMEM),
            pl.BlockSpec((devices, block_rows, 128), lambda k: (0, 0, 0)),
            pl.BlockSpec((S_STEP, rows, lat_total), lambda k: (k, 0, 0)),
        ],
        out_specs=pl.BlockSpec((owners, S_STEP, lat_rows, 128), lambda k: (0, k, 0, 0)),
        out_shape=jax.ShapeDtypeStruct((owners, slots, lat_rows, 128), BF16),
        scratch_shapes=[
            pltpu.VMEM(((devices + 1) * block_rows, 128), F32),
            pltpu.VMEM((S_STEP, degrees + 8, 128), F32),
            pltpu.VMEM((S_STEP, lat_total, 128), F32),
        ],
        compiler_params=params(24),
        cost_estimate=cost(7),
        name="synthesis",
    )(*places, filtered, basis)


HELD = 48
OWNER_UNROLL = 2


def filter_body(slots, me_ref, in_ref, weight_ref, out_ref, degree_ref, rows_ref, kept_ref, tight_ref):
    devices, block_rows, _ = in_ref.shape
    owners = devices // 8

    def gather(owner, _):
        start = pl.multiple_of(owner * HELD, 8)
        for half in range(2):
            lanes = slice(128 * half, 128 * half + 128)
            tiles = [in_ref[owner * 8 + 4 * half + a].astype(F32) for a in range(4)]
            for hj, tile in enumerate(swap_groups(tiles)):
                rows_ref[hj, half, pl.ds(start, block_rows), :] = tile
                rows_ref[hj, half, pl.ds(start + block_rows, HELD - block_rows), :] = jnp.zeros(
                    (HELD - block_rows, 128), F32
                )
        return 0

    lax.fori_loop(0, owners, gather, 0, unroll=OWNER_UNROLL)
    per_owner = HELD // 3
    for s in range(3):
        weights = weight_ref[:, s, 0].reshape(256, 256)
        for hj in range(4):
            table = [
                rows_ref[hj, half, pl.ds(s, owners * per_owner, stride=3), :] for half in range(2)
            ]
            for half in range(2):
                for i in range(owners):
                    row = (hj * owners + i) * slots
                    tight_ref[row : row + slots, 128 * half : 128 * half + 128] = table[half][
                        per_owner * i : per_owner * i + slots
                    ]
            whole = jnp.concatenate([half.astype(BF16) for half in table], axis=1)
            product = nt_dot(whole, weights)
            for half in range(2):
                kept_ref[hj, half, pl.ds(s, owners * per_owner, stride=3), :] = product[
                    :, 128 * half : 128 * half + 128
                ]
        degree_ref[s] = tight_ref[...].astype(BF16)

    def scatter(owner, _):
        start = pl.multiple_of(owner * HELD, 8)
        for half in range(2):
            tiles = [kept_ref[hj, half, pl.ds(start, block_rows), :] for hj in range(4)]
            for a, tile in enumerate(swap_groups(tiles)):
                out_ref[owner * 8 + 4 * half + a] = tile.astype(BF16)
        return 0

    lax.fori_loop(0, owners, scatter, 0, unroll=OWNER_UNROLL)


def spectral_filter(received, weights, me, slots):
    devices, block_rows, _ = received.shape
    owners = devices // 8
    whole = lambda shape: pl.BlockSpec(shape, lambda n, me_ref: (0,) * len(shape))
    degree_shape = (3, 4 * owners * slots, 256)
    return pl.pallas_call(
        functools.partial(filter_body, slots),
        grid_spec=pltpu.PrefetchScalarGridSpec(
            num_scalar_prefetch=1,
            grid=(1,),
            in_specs=[
                whole(received.shape),
                pl.BlockSpec((8, 3, 1, GROUP, 256), lambda n, me_ref: (0, 0, me_ref[0], 0, 0)),
            ],
            out_specs=[whole(received.shape), whole(degree_shape)],
            scratch_shapes=[
                pltpu.VMEM((4, 2, owners * HELD + 8, 128), F32),
                pltpu.VMEM((4, 2, owners * HELD + 8, 128), F32),
                pltpu.VMEM((4 * owners * slots, 256), F32),
            ],
        ),
        out_shape=[
            jax.ShapeDtypeStruct(received.shape, BF16),
            jax.ShapeDtypeStruct(degree_shape, BF16),
        ],
        compiler_params=params(22),
        cost_estimate=cost(6),
        name="spectral_filter",
    )(me, received, weights)


def grad_body(in_ref, degree_ref, out_ref, rows_ref):
    step = pl.program_id(0)
    owners, slots, part, _ = in_ref.shape

    @pl.when(step == 0)
    def _():
        rows_ref[: owners * slots * part, :] = in_ref[...].astype(F32).reshape(-1, 128)

    group = lax.broadcasted_iota(jnp.int32, (owners * slots, 128), 1) // GROUP
    for j in range(8):
        grad = rows_ref[pl.ds(8 * step + j, owners * slots, stride=part), :]
        spread = [jnp.where(group == hj, grad, 0.0).astype(BF16) for hj in range(4)]
        sums = tn_dot(jnp.concatenate(spread, axis=0), degree_ref[j, 0])
        total = sums[:GROUP] + sums[GROUP : 2 * GROUP]
        out_ref[j] = total + (sums[2 * GROUP : 3 * GROUP] + sums[3 * GROUP :])


def filter_grad(received, by_degree):
    owners, slots, part, _ = received.shape
    chans, steps, rows, _ = by_degree.shape
    return pl.pallas_call(
        grad_body,
        grid=(steps,),
        in_specs=[
            pl.BlockSpec(received.shape, lambda s: (0, 0, 0, 0)),
            pl.BlockSpec((chans, 1, rows, 256), lambda s: (0, s, 0, 0)),
        ],
        out_specs=pl.BlockSpec((chans, GROUP, 256), lambda s: (s, 0, 0)),
        out_shape=jax.ShapeDtypeStruct((part, GROUP, 256), F32),
        scratch_shapes=[pltpu.VMEM(((owners * slots + 1) * part, 128), F32)],
        compiler_params=params(40),
        cost_estimate=cost(6),
        name="filter_grad",
    )(received, by_degree)


def stay(array):
    return pltpu.with_memory_space_constraint(array, pltpu.HBM)


def exchange(array, axis):
    return lax.all_to_all(array, axis, split_axis=0, concat_axis=0, tiled=True)


def on_device(grid_in, lat_weights, legendre_basis, pair_list, filter_weights, cotangent):
    owners = lax.axis_size("lat")
    chans = lax.axis_size("chan")
    slots, rows, _ = legendre_basis.shape
    degrees = rows - 1
    _, lat_rows, chan_rows, lon_count = grid_in.shape
    grid, cotangent = grid_in[0], cotangent[0]
    owner = lax.axis_index("lat").reshape(1).astype(jnp.int32)
    me = lax.axis_index("chan").reshape(1).astype(jnp.int32)
    places = (owner, pair_list)
    table = longitude_table(degrees, lon_count, False)
    inverse_table = longitude_table(degrees, lon_count, True)

    everyone = ("lat", "chan")
    spectrum, weights = forward_transform(
        grid, lat_weights, pair_list, table, filter_weights, owner, owners, slots
    )
    weights = lax.all_gather(weights, "chan")
    weights = weights.reshape(chans, degrees // owners // chans, chans, chan_rows, -1)
    coefficients = analysis(exchange(spectrum, "lat"), stay(legendre_basis), places, True)
    filtered, by_degree = spectral_filter(exchange(coefficients, everyone), weights, me, slots)
    filtered, by_degree = lax.optimization_barrier((exchange(filtered, everyone), by_degree))
    by_degree = lax.all_gather(by_degree, "chan")
    lines = synthesize(filtered, stay(legendre_basis), places, owners, lat_rows)
    gate, grads = middle_transform(
        exchange(lines, "lat"), cotangent, pair_list, inverse_table, owners, slots
    )
    grads = analysis(exchange(grads, "lat"), legendre_basis, places, False)
    weight_grad = filter_grad(exchange(grads, "lat"), stay(by_degree))
    block_out = (grid.astype(F32) + gate.astype(F32)).astype(BF16)
    return (block_out[None], weight_grad)


def solution(mesh):
    in_specs = (
        P(None, "lat", "chan", None),
        P("lat"),
        P("lat", None, None),
        P(),
        P(None, "chan", None),
        P(None, "lat", "chan", None),
    )
    out_specs = (P(None, "lat", "chan", None), P("lat", "chan", None))
    return jax.shard_map(
        on_device, mesh=mesh, in_specs=in_specs, out_specs=out_specs, check_vma=False
    )
```
